32 devices in a mesh: region: 8 (over z, x), tm: 4 (over y, core).
Axes of the slice: x: 2, y: 2, z: 4, core: 2. Of those that a mesh axis runs over, the one named last changes fastest.
Arguments:
- tensor: bfloat16 [2048, 32, 2, 128], P('region'), may hold values from -6 to 6
- g_occ: bfloat16 [4, 1024, 128], P('tm', 'region'), may hold values from -0.375 to 0.375
- g_virt: bfloat16 [4, 1024, 128], P('tm', 'region'), may hold values from -0.375 to 0.375
- offsets: int32 [8, 2], P('region'), may hold values from -1 to 1, as said below
- pattern: int32 [8, 3], P('region'), may hold values from 0 to 1, as said below
Outputs:
- screened: float32 [4, 2048, 768], P('tm', 'region')
The draws below stay inside these ranges and needn't reach their ends.
Inputs may be any that keep to these rules, and one draw needn't show every extreme that they name: Row r holds 2 distinct offsets in increasing order, and r + offset lies within 0 to 7. `pattern`: row r is (b[r-1], 1, b[r]) for bond bits b with b[-1] = b[7] = 0, so that the kept blocks are symmetric.
All inputs are finite; a program needn't handle non-finite values.
Results may differ from the reference program's by a relative error of at most 0.0039.
Values may be sent and summed in bfloat16 or wider, within the bound.
No kernel may reach another device: no remote copies, remote signals or barrier semaphores. Data moves between devices by JAX's collectives and lax.ppermute only.
A program may use at most 64 MiB of HBM per device.

```python
import math
import jax
import jax.numpy as jnp
from jax import lax

MU = 32
NU = 128
LAM = 128
KB = 2
ROWS = 256
NREG = 8
NTIME = 4
ORB = 1024
NAUX = 2048


def draw_offsets(key, part):
    omitted = jax.random.randint(key, (NREG,), 0, 3)
    places = jnp.arange(NREG)
    omitted = jnp.where(places == 0, 0, omitted)
    omitted = jnp.where(places == NREG - 1, 2, omitted)
    first_off = jnp.where(omitted == 0, 1, 0)
    second = jnp.where(omitted == 2, 1, 2)
    return (jnp.stack([first_off, second], 1) - 1).astype(jnp.int32)


def draw_pattern(key, part):
    bond_bits = jax.random.randint(jax.random.fold_in(key, 7), (NREG,), 0, 2)
    places = jnp.arange(NREG)
    bond_bits = jnp.where(places == NREG - 1, 0, bond_bits)
    earlier = jnp.concatenate([jnp.zeros((1,), bond_bits.dtype), bond_bits[:-1]])
    return jnp.stack([earlier, jnp.ones_like(bond_bits), bond_bits], 1).astype(jnp.int32)


def shard_levels(key, shape, split, smallest, top_value):
    level = 1.0
    for axis_at, parts in split:
        draws = jax.random.uniform(jax.random.fold_in(jax.random.fold_in(key, 6), axis_at), (parts,), jnp.float32, smallest / len(split), top_value / len(split))
        level = level * jnp.repeat(jnp.exp(draws), shape[axis_at] // parts).reshape((-1,) + (1,) * (len(shape) - 1 - axis_at))
    return level


def gaussian(stream_key, dims, spread, most, split=(), kind=jnp.bfloat16):
    result = jax.random.normal(stream_key, dims, jnp.float32) * spread
    if len(split) > 0:
        result = shard_levels(stream_key, dims, split, -0.22, 0.18) * result
    return jnp.clip(result, min=-most, max=most).astype(kind)


def setup_inputs(seed: int = 0) -> dict:
    keys = jax.random.split(jax.random.key(seed), 6)
    return {
        "tensor": gaussian(keys[0], (NAUX, MU, KB, NU), 1.0, 6.0, ((0, 8),)),
        "g_occ": gaussian(keys[1], (NTIME, ORB, LAM), (KB * NU) ** -0.5, 0.375, ((0, 4), (1, 8))),
        "g_virt": gaussian(keys[2], (NTIME, ORB, LAM), (KB * NU) ** -0.5, 0.375, ((0, 4), (1, 8))),
        "offsets": draw_offsets(jax.random.fold_in(keys[5], 71), 0),
        "pattern": draw_pattern(jax.random.fold_in(keys[5], 71), 0),
    }


time_points = (0.1, 0.5, 1.5, 4.0)
time_weights = (0.2, 0.6, 1.2, 2.5)
omega_points = (0.2, 0.9, 2.5, 7.0)

def cosine_table():
    points = jnp.array(time_points, jnp.float32)
    weights = jnp.array(time_weights, jnp.float32)
    omegas = jnp.array(omega_points, jnp.float32)
    return weights[None, :] * jnp.cos(omegas[:, None] * points[None, :])

def contract(first_op, second_op):
    return lax.dot_general(first_op, second_op, (((1,), (1,)), ((), ())), preferred_element_type=jnp.float32)

def shifted(stacked):
    padding = jnp.zeros_like(stacked[:1])
    previous = jnp.concatenate([padding, stacked[:-1]], 0)
    following = jnp.concatenate([stacked[1:], padding], 0)
    return (previous, following)

def rotate_all(tensor, green, offsets):
    blocks = green.reshape(NREG, NU, 2 * LAM)
    previous, following = shifted(blocks)
    nearby = jnp.stack([previous, blocks, following], 1)
    picked = jnp.take_along_axis(nearby, (offsets + 1).astype(jnp.int32)[:, :, None, None], axis=1)
    tensor_rows = tensor.reshape(NREG, ROWS * MU, KB * NU)

    def per_region(inputs):
        tensor_slab, chosen = inputs
        product = jnp.dot(tensor_slab, chosen.reshape(KB * NU, 2 * LAM), preferred_element_type=jnp.float32)
        product = product.reshape(ROWS, MU, 2, LAM)
        occupied = product[:, :, 0].reshape(ROWS, MU * LAM).astype(jnp.bfloat16)
        virtual = product[:, :, 1].reshape(ROWS, MU * LAM).astype(jnp.bfloat16)
        return (occupied, virtual)
    return lax.map(per_region, (tensor_rows, picked))

def polarize(occupied, virtual, pattern, prefactor):
    occ_prev, occ_next = shifted(occupied)
    virt_prev, virt_next = shifted(virtual)

    def per_region(region_items):
        own_occ, own_virt, prev_occ, prev_virt, next_occ, next_virt, pattern_row = region_items
        mask_weights = pattern_row.astype(jnp.float32)
        left_block = prefactor * (contract(own_occ, prev_virt) + contract(own_virt, prev_occ)) * mask_weights[0]
        middle = prefactor * (contract(own_occ, own_virt) + contract(own_virt, own_occ))
        right_block = prefactor * (contract(own_occ, next_virt) + contract(own_virt, next_occ)) * mask_weights[2]
        return jnp.concatenate([left_block, middle, right_block], 1)
    return lax.map(per_region, (occupied, virtual, occ_prev, virt_prev, occ_next, virt_next, pattern))

def column_block(matrix, position):
    extent = matrix.shape[0]
    return matrix[:, (position + 1) * extent:(position + 2) * extent]

def combine(center_rows, below_rows, above_rows, mask_weights):
    sources = (below_rows, center_rows, above_rows)
    pieces = []
    for target in (-1, 0, 1):
        summed = column_block(center_rows, target)
        for middle in (-1, 0, 1):
            if abs(target - middle) <= 1:
                summed = summed + jnp.dot(column_block(center_rows, middle), column_block(sources[middle + 1], target - middle), precision=lax.Precision.HIGHEST, preferred_element_type=jnp.float32)
        pieces.append(summed * mask_weights[target + 1])
    return jnp.concatenate(pieces, 1)

def screen(freq_rows, pattern):
    previous, following = shifted(freq_rows)

    def per_region(region_items):
        center_rows, below_rows, above_rows, pattern_row = region_items
        return combine(center_rows, below_rows, above_rows, pattern_row.astype(jnp.float32))
    return lax.map(per_region, (freq_rows, previous, following, pattern))

def reference(tensor, g_occ, g_virt, offsets, pattern):
    prefactor = 1.0 / math.sqrt(2.0 * MU * LAM) / (3.0 * ROWS) ** 0.25
    cos_table = cosine_table()
    per_time = []
    for moment in range(NTIME):
        green = jnp.concatenate([g_occ[moment], g_virt[moment]], 1)
        occupied, virtual = rotate_all(tensor, green, offsets)
        per_time.append(polarize(occupied, virtual, pattern, prefactor))
    results = []
    for freq_index in range(NTIME):
        summed = cos_table[freq_index, 0] * per_time[0]
        for moment in range(1, NTIME):
            summed = summed + cos_table[freq_index, moment] * per_time[moment]
        results.append(screen(summed, pattern))
    return jnp.stack(results, 0).reshape(NTIME, NAUX, 3 * ROWS)
```

```python
import functools
import math

import jax
import jax.numpy as jnp
import numpy as np
from jax import lax
from jax.experimental import pallas as pl
from jax.experimental.pallas import tpu as pltpu
from jax.sharding import PartitionSpec as P

time_points = (0.1, 0.5, 1.5, 4.0)
time_weights = (0.2, 0.6, 1.2, 2.5)
omega_points = (0.2, 0.9, 2.5, 7.0)

f32, bf16 = jnp.float32, jnp.bfloat16
VMEM_BYTES = 40 * 2**20


def cosine_table():
    points = np.array(time_points, np.float32)
    weights = np.array(time_weights, np.float32)
    omegas = np.array(omega_points, np.float32)
    return weights[None, :] * np.cos(omegas[:, None] * points[None, :])


def shift(block, distance):
    devices = range(lax.axis_size("region"))
    route = [(i - distance, i) for i in devices if i - distance in devices]
    return lax.ppermute(block, "region", route)


def partner(block, bit):
    return lax.ppermute(block, "tm", [(i, i ^ bit) for i in range(lax.axis_size("tm"))])


def mm(a, b):
    return jnp.dot(a, b, preferred_element_type=f32)


def mm_nt(a, b):
    return lax.dot_general(a, b, (((1,), (1,)), ((), ())), preferred_element_type=f32)


def spec_all(count):
    return [pl.BlockSpec(memory_space=pltpu.VMEM)] * count


SMEM = pl.BlockSpec(memory_space=pltpu.SMEM)


def relayout_kernel(mus, kb, x_ref, out_ref, wide):
    wide[...] = x_ref[...].astype(f32)
    rows = out_ref.shape[1]
    nu = x_ref.shape[1]
    for mu in range(mus):
        for k in range(kb):
            part = wide[pl.ds(mu * kb + k, rows, stride=mus * kb), :]
            out_ref[mu, :, k * nu : (k + 1) * nu] = part.astype(bf16)


def relayout(tensor, steps):
    rows, mus, kb, nu = tensor.shape
    part = rows // steps
    return pl.pallas_call(
        functools.partial(relayout_kernel, mus, kb),
        grid=(steps,),
        out_shape=jax.ShapeDtypeStruct((mus, rows, kb * nu), bf16),
        in_specs=[pl.BlockSpec((part * mus * kb, nu), lambda i: (i, 0))],
        out_specs=pl.BlockSpec((mus, part, kb * nu), lambda i: (0, i, 0)),
        scratch_shapes=[pltpu.VMEM((part * mus * kb, nu), f32)],
        compiler_params=pltpu.CompilerParams(vmem_limit_bytes=VMEM_BYTES),
        cost_estimate=pl.CostEstimate(flops=0, bytes_accessed=4 * tensor.size, transcendentals=0),
        name="relayout",
    )(tensor.reshape(rows * mus * kb, nu))


def weights_kernel(n, where, table, *refs):
    greens, (center_ref, right_ref, terms) = refs[:n], refs[n:]
    nu = greens[0].shape[1] // 2
    me = where[0]
    own = [where[1 + s] + 1 for s in range(2)]
    following = [where[3 + s] + 2 for s in range(2)]

    def pick(green, places):
        occ = jnp.concatenate([green[p, :nu, :] for p in places], 0)
        virt = jnp.concatenate([green[p, nu:, :] for p in places], 0)
        return jnp.concatenate([occ, virt], 1), jnp.concatenate([virt, occ], 1)

    center = None
    for i in range(n):
        first, first_swapped = pick(greens[i], own)
        _, second_swapped = pick(greens[i], following)
        term = table[me, me ^ i] * mm_nt(first, first_swapped)
        center = term if center is None else center + term
        terms[i] = mm_nt(second_swapped, first)
    center_ref[...] = center.astype(bf16)
    size = center_ref.shape[0]
    for q in range(n):
        total = table[me ^ q, me] * terms[0]
        for i in range(1, n):
            total = total + table[me ^ q, me ^ i] * terms[i]
        right_ref[:, q * size : (q + 1) * size] = total.astype(bf16)


def weights(where, greens):
    n = len(greens)
    size = 2 * greens[0].shape[1] // 2
    return pl.pallas_call(
        functools.partial(weights_kernel, n),
        out_shape=[
            jax.ShapeDtypeStruct((size, size), bf16),
            jax.ShapeDtypeStruct((size, n * size), bf16),
        ],
        in_specs=[SMEM, SMEM] + spec_all(n),
        out_specs=spec_all(2),
        scratch_shapes=[pltpu.VMEM((n, size, size), f32)],
        compiler_params=pltpu.CompilerParams(vmem_limit_bytes=VMEM_BYTES),
        cost_estimate=pl.CostEstimate(
            flops=4 * n * size**3, bytes_accessed=n * size**2 * 4, transcendentals=0
        ),
        name="weights",
    )(where, jnp.asarray(cosine_table()), *greens)


def center_kernel(scale, rows_ref, weight_ref, out_ref, low_ref, total):
    step = pl.program_id(0)
    mus, rows, width = rows_ref.shape
    turned = mm(rows_ref[...].reshape(mus * rows, width), weight_ref[...]).astype(bf16)
    acc = mm_nt(rows_ref[0], turned[:rows])
    for mu in range(1, mus):
        acc = acc + mm_nt(rows_ref[mu], turned[mu * rows : (mu + 1) * rows])

    @pl.when(step == 0)
    def _():
        total[...] = acc

    @pl.when(step > 0)
    def _():
        total[...] += acc

    @pl.when(step == pl.num_programs(0) - 1)
    def _():
        out_ref[...] = scale * total[...]
        low_ref[...] = (scale * total[...]).astype(bf16)


def center_block(scale, turned_rows, weight, steps):
    mus, rows, width = turned_rows.shape
    part = mus // steps
    return pl.pallas_call(
        functools.partial(center_kernel, scale),
        grid=(steps,),
        out_shape=[
            jax.ShapeDtypeStruct((rows, rows), f32),
            jax.ShapeDtypeStruct((rows, rows), bf16),
        ],
        in_specs=[
            pl.BlockSpec((part, rows, width), lambda i: (i, 0, 0)),
            pl.BlockSpec((width, width), lambda i: (0, 0)),
        ],
        out_specs=[pl.BlockSpec((rows, rows), lambda i: (0, 0))] * 2,
        scratch_shapes=[pltpu.VMEM((rows, rows), f32)],
        compiler_params=pltpu.CompilerParams(vmem_limit_bytes=VMEM_BYTES),
        cost_estimate=pl.CostEstimate(
            flops=2 * mus * rows * width * (width + rows),
            bytes_accessed=2 * mus * rows * width,
            transcendentals=0,
        ),
        name="center",
    )(turned_rows, weight)


def right_kernel(n, mus, kb, steps, first, last, scale, *refs):
    far_ref, weight_ref, rows_ref = refs[:3]
    refs = refs[3:]
    if not first:
        before_ref, refs = refs[0], refs[1:]
    outs, (wide, total) = refs[:-2], refs[-2:]
    step = pl.program_id(0)
    part = mus // steps
    nu = far_ref.shape[1]
    cols = far_ref.shape[0] // (mus * kb)
    width = kb * nu

    @pl.when(step == 0)
    def _():
        wide[...] = far_ref[...].astype(f32)
        if first:
            total[...] = jnp.zeros_like(total)
        else:
            total[...] = before_ref[...]

    pieces = []
    for mu in range(part):
        line = [
            wide[pl.ds((step * part + mu) * kb + k, cols, stride=mus * kb), :] for k in range(kb)
        ]
        pieces.append(jnp.concatenate(line, 1).astype(bf16))
    turned = mm(jnp.concatenate(pieces, 0), weight_ref[...]).astype(bf16)
    acc = total[...]
    for mu in range(part):
        rows = turned[mu * cols : (mu + 1) * cols]
        stacked = jnp.concatenate([rows[:, q * width : (q + 1) * width] for q in range(n)], 0)
        acc = acc + mm_nt(stacked, rows_ref[mu])
    total[...] = acc

    @pl.when(step == steps - 1)
    def _():
        if last:
            for q in range(n):
                outs[q][...] = (scale * total[q * cols : (q + 1) * cols, :]).astype(bf16)
        else:
            outs[0][...] = total[...]


def right_part(scale, far, weight, turned_rows, before, chunk, last, steps):
    cols, mus, kb, nu = far.shape
    _, rows, width = turned_rows.shape
    n = weight.shape[1] // width
    part = mus // steps
    first = before is None
    whole = lambda *shape: pl.BlockSpec(shape, lambda i: (0,) * len(shape))
    operands = [far.reshape(cols * mus * kb, nu), weight, turned_rows]
    in_specs = [
        whole(cols * mus * kb, nu),
        whole(width, n * width),
        pl.BlockSpec((part, rows, width), lambda i: (chunk * steps + i, 0, 0)),
    ]
    if not first:
        operands.append(before)
        in_specs.append(whole(n * cols, rows))
    if last:
        out_shape = [jax.ShapeDtypeStruct((cols, rows), bf16)] * n
        out_specs = [whole(cols, rows)] * n
    else:
        out_shape = [jax.ShapeDtypeStruct((n * cols, rows), f32)]
        out_specs = [whole(n * cols, rows)]
    return pl.pallas_call(
        functools.partial(right_kernel, n, mus, kb, steps, first, last, scale),
        grid=(steps,),
        out_shape=out_shape,
        in_specs=in_specs,
        out_specs=out_specs,
        scratch_shapes=[
            pltpu.VMEM((cols * mus * kb, nu), f32),
            pltpu.VMEM((n * cols, rows), f32),
        ],
        compiler_params=pltpu.CompilerParams(vmem_limit_bytes=VMEM_BYTES),
        cost_estimate=pl.CostEstimate(
            flops=2 * mus * cols * n * width * (width + rows),
            bytes_accessed=2 * mus * rows * width,
            transcendentals=0,
        ),
        name="right",
    )(*operands)


def split(value):
    high = value.astype(bf16)
    return high, (value - high.astype(f32)).astype(bf16)


def screen_kernel(n, where, center_ref, below_ref, above_ref, left_ref, *refs):
    pieces, (out_ref, left, right_t) = refs[:n], refs[n:]
    me = where[0]
    cols = pieces[0].shape[0]
    size = center_ref.shape[0]
    for i in range(n):
        start = pl.multiple_of((me ^ i) * cols, cols)
        left[pl.ds(start, cols), :] = left_ref[i]
        right_t[pl.ds(start, cols), :] = pieces[i][...]
    masks = [where[1 + e].astype(f32) for e in range(3)]
    lower = left[...] * masks[0].astype(bf16)
    upper = right_t[...].T * masks[2].astype(bf16)
    center = center_ref[...]
    high, low = split(center)
    out_ref[0, :, :size] = masks[0] * (
        lower.astype(f32) + mm(lower, below_ref[...]) + mm(high, lower) + mm(low, lower)
    )
    out_ref[0, :, size : 2 * size] = masks[1] * (
        center
        + mm_nt(lower, lower)
        + mm_nt(upper, upper)
        + mm(high, high)
        + mm(high, low)
        + mm(low, high)
    )
    out_ref[0, :, 2 * size :] = masks[2] * (
        upper.astype(f32) + mm(upper, above_ref[...]) + mm(high, upper) + mm(low, upper)
    )


def screen(where, center, below, above, left, pieces):
    n = len(pieces)
    size = center.shape[0]
    return pl.pallas_call(
        functools.partial(screen_kernel, n),
        out_shape=jax.ShapeDtypeStruct((1, size, 3 * size), f32),
        in_specs=[SMEM] + spec_all(4 + n),
        out_specs=pl.BlockSpec(memory_space=pltpu.VMEM),
        scratch_shapes=[pltpu.VMEM((size, size), bf16)] * 2,
        compiler_params=pltpu.CompilerParams(vmem_limit_bytes=VMEM_BYTES),
        cost_estimate=pl.CostEstimate(
            flops=22 * size**3, bytes_accessed=16 * size**2, transcendentals=0
        ),
        name="screen",
    )(where, center, below, above, left, *pieces)


def local(tensor, g_occ, g_virt, offsets, pattern):
    rows, mus, kb, nu = tensor.shape
    lam = g_occ.shape[2]
    n = lax.axis_size("tm")
    assert n & (n - 1) == 0 and rows % n == 0
    me = lax.axis_index("tm")
    scale = 1.0 / math.sqrt(2.0 * mus * lam) / (3.0 * rows) ** 0.25
    cols = rows // n
    chunks = 2
    far = []
    for c in range(chunks):
        start = (me * cols, c * (mus // chunks), 0, 0)
        slab = lax.dynamic_slice(tensor, start, (cols, mus // chunks, kb, nu))
        far.append(shift(slab, -1))

    note = jnp.zeros((16, lam), bf16).at[:1, :kb].set(offsets.astype(bf16))
    parcel = jnp.concatenate([g_occ[0], g_virt[0], note], 0)
    size = 2 * nu
    above, below, second = shift(parcel, -1), shift(parcel, 1), shift(parcel, -2)
    stack = jnp.stack([below[:size], parcel[:size], above[:size], second[:size]], 0)
    next_offsets = above[size, :kb].astype(jnp.int32)
    greens = {0: stack}
    bit = n // 2
    while bit:
        for i in list(greens):
            greens[i ^ bit] = partner(greens[i], bit)
        bit //= 2
    where = jnp.concatenate([me[None].astype(jnp.int32), offsets[0], next_offsets])
    center_weight, right_weight = weights(where, [greens[i] for i in range(n)])

    turned_rows = relayout(tensor, 8)
    center, center_low = center_block(scale, turned_rows, center_weight, 4)
    center_below, center_above = shift(center_low, 1), shift(center_low, -1)

    before = None
    for c in range(chunks):
        last = c == chunks - 1
        parts = right_part(scale, far[c], right_weight, turned_rows, before, c, last, 2)
        before = parts[0]
    pieces = [parts[0]] + [partner(parts[i], i) for i in range(1, n)]
    left = shift(jnp.stack(pieces, 0), 1)
    places = jnp.concatenate([me[None].astype(jnp.int32), pattern[0]])
    return screen(places, center, center_below, center_above, left, pieces)


def solution(mesh):
    return jax.shard_map(
        local,
        mesh=mesh,
        in_specs=(
            P("region", None, None, None),
            P("tm", "region", None),
            P("tm", "region", None),
            P("region", None),
            P("region", None),
        ),
        out_specs=P("tm", "region", None),
        check_vma=False,
    )
```

```python
import functools
import math

import jax
import jax.numpy as jnp
import numpy as np
from jax import lax
from jax.experimental import pallas as pl
from jax.experimental.pallas import tpu as pltpu
from jax.sharding import PartitionSpec as P

time_points = (0.1, 0.5, 1.5, 4.0)
time_weights = (0.2, 0.6, 1.2, 2.5)
omega_points = (0.2, 0.9, 2.5, 7.0)

f32, bf16 = jnp.float32, jnp.bfloat16
VMEM_BYTES = 24 * 2**20
PREPARE_BYTES = 60 * 2**20
RELAYOUT_BYTES = 56 * 2**20
TILE = 16


def cosine_table():
    points = np.array(time_points, np.float32)
    weights = np.array(time_weights, np.float32)
    omegas = np.array(omega_points, np.float32)
    return weights[None, :] * np.cos(omegas[:, None] * points[None, :])


def shift(block, distance):
    devices = range(lax.axis_size("region"))
    route = [(i - distance, i) for i in devices if i - distance in devices]
    return lax.ppermute(block, "region", route)


def partner(block, bit):
    return lax.ppermute(block, "tm", [(i, i ^ bit) for i in range(lax.axis_size("tm"))])


def mm(a, b):
    return jnp.dot(a, b, preferred_element_type=f32)


def mm_nt(a, b):
    return lax.dot_general(a, b, (((1,), (1,)), ((), ())), preferred_element_type=f32)


def spec_all(count):
    return [pl.BlockSpec(memory_space=pltpu.VMEM)] * count


SMEM = pl.BlockSpec(memory_space=pltpu.SMEM)
HBM = pl.BlockSpec(memory_space=pltpu.HBM)


def swap_matrix(tile):
    size = tile * tile
    to = lax.broadcasted_iota(jnp.int32, (size, size), 0)
    of = lax.broadcasted_iota(jnp.int32, (size, size), 1)
    return (of == (to % tile) * tile + to // tile).astype(f32).astype(bf16)


def turn(source, lead, rows, lines, put):
    swap = swap_matrix(TILE)
    places = [(r, c) for r in range(0, rows, TILE) for c in range(0, lines, TILE)]
    for at in range(0, len(places), 2):
        pair = places[at : at + 2]
        blocks = [
            jnp.concatenate([source(lead + r + i, c) for i in range(TILE)], 0) for r, c in pair
        ]
        width = blocks[0].shape[1]
        moved = mm(swap, jnp.concatenate(blocks, 1)).astype(bf16)
        for h, (r, c) in enumerate(pair):
            for i in range(TILE):
                put(c + i, r, moved[i * TILE : (i + 1) * TILE, h * width : (h + 1) * width])


def relayout_kernel(kb, chunks, x_ref, out_ref, buffer, sems):
    rows, lines, nu = x_ref.shape
    part = rows // chunks
    copies = [
        pltpu.make_async_copy(
            x_ref.at[pl.ds(c * part, part)], buffer.at[pl.ds(c * part, part)], sems.at[c]
        )
        for c in range(chunks)
    ]
    for copy in copies:
        copy.start()
    for c in range(chunks):
        copies[c].wait()

        def put(line, row, value):
            k = line % kb
            start = c * part + row
            out_ref[line // kb, start : start + TILE, k * nu : (k + 1) * nu] = value

        turn(lambda r, l: buffer[r, l : l + TILE, :], c * part, part, lines, put)


def relayout(lined, kb, chunks):
    rows, lines, nu = lined.shape
    return pl.pallas_call(
        functools.partial(relayout_kernel, kb, chunks),
        out_shape=jax.ShapeDtypeStruct((lines // kb, rows, kb * nu), bf16),
        in_specs=[HBM],
        out_specs=pl.BlockSpec(memory_space=pltpu.VMEM),
        scratch_shapes=[
            pltpu.VMEM((rows, lines, nu), bf16),
            pltpu.SemaphoreType.DMA((chunks,)),
        ],
        compiler_params=pltpu.CompilerParams(vmem_limit_bytes=RELAYOUT_BYTES),
        cost_estimate=pl.CostEstimate(flops=0, bytes_accessed=0, transcendentals=0),
        name="relayout",
    )(lined)


def prepare_kernel(first, where, offsets_ref, x_ref, occ_ref, virt_ref, head_ref, tail_ref, green_ref, offsets, sems):
    cols = tail_ref.shape[0]
    notes = head_ref.shape[0] - cols
    blocks = occ_ref.shape[0]
    lines = x_ref.shape[1]
    rows = pl.ds(where[0] * cols, cols)
    moves = [
        (offsets_ref, offsets),
        (x_ref.at[rows, pl.ds(0, first)], head_ref.at[pl.ds(notes, cols)]),
        (x_ref.at[rows, pl.ds(first, lines - first)], tail_ref),
    ]
    for ref in (head_ref, green_ref):
        moves.append((occ_ref, ref.at[pl.ds(0, blocks)]))
        moves.append((virt_ref, ref.at[pl.ds(blocks, blocks)]))
    copies = [pltpu.make_async_copy(*move, sems.at[i]) for i, move in enumerate(moves)]
    for copy in copies:
        copy.start()
    copies[0].wait()
    shape = head_ref.shape[1:]
    line = lax.broadcasted_iota(jnp.int32, shape, 0)
    values = jnp.where(line < shape[0] // 2, offsets[0, 0], offsets[0, 1])
    head_ref[2 * blocks] = values.astype(f32).astype(bf16)
    for copy in copies[1:]:
        copy.wait()


def prepare(where, offsets, lined, occ, virt, first, n):
    rows, lines, nu = lined.shape
    blocks = occ.shape[0]
    cols = rows // n
    return pl.pallas_call(
        functools.partial(prepare_kernel, first),
        out_shape=[
            jax.ShapeDtypeStruct((2 * blocks + 1 + cols, first, nu), bf16),
            jax.ShapeDtypeStruct((cols, lines - first, nu), bf16),
            jax.ShapeDtypeStruct((2 * blocks, TILE, nu), bf16),
        ],
        in_specs=[SMEM] + [HBM] * 4,
        out_specs=spec_all(3),
        scratch_shapes=[pltpu.SMEM(offsets.shape, jnp.int32), pltpu.SemaphoreType.DMA((7,))],
        compiler_params=pltpu.CompilerParams(vmem_limit_bytes=PREPARE_BYTES),
        cost_estimate=pl.CostEstimate(flops=0, bytes_accessed=0, transcendentals=0),
        name="prepare",
    )(where, offsets, lined, occ, virt)


def weights_kernel(n, place, where, offsets, table, head_ref, *refs):
    greens, (center_ref, right_ref, terms) = refs[:n], refs[n:]
    nu = greens[0].shape[1] // 2
    me = where[0]
    note = head_ref[place].astype(f32)
    half = note.shape[0] // 2
    told = [jnp.max(note[:half]), jnp.max(note[half:])]
    own = [offsets[0, s] + 1 for s in range(2)]
    following = [told[s].astype(jnp.int32) + 2 for s in range(2)]

    def pick(green, places):
        occ = jnp.concatenate([green[p, :nu, :] for p in places], 0)
        virt = jnp.concatenate([green[p, nu:, :] for p in places], 0)
        return jnp.concatenate([occ, virt], 1), jnp.concatenate([virt, occ], 1)

    center = None
    for i in range(n):
        first, first_swapped = pick(greens[i], own)
        _, second_swapped = pick(greens[i], following)
        term = table[me, me ^ i] * mm_nt(first, first_swapped)
        center = term if center is None else center + term
        terms[i] = mm_nt(second_swapped, first)
    center_ref[...] = center.astype(bf16)
    size = center_ref.shape[0]
    for q in range(n):
        total = table[me ^ q, me] * terms[0]
        for i in range(1, n):
            total = total + table[me ^ q, me ^ i] * terms[i]
        right_ref[:, q * size : (q + 1) * size] = total.astype(bf16)


def weights(where, offsets, head, place, greens):
    n = len(greens)
    size = 2 * greens[0].shape[1] // 2
    return pl.pallas_call(
        functools.partial(weights_kernel, n, place),
        out_shape=[
            jax.ShapeDtypeStruct((size, size), bf16),
            jax.ShapeDtypeStruct((size, n * size), bf16),
        ],
        in_specs=[SMEM, SMEM, SMEM] + spec_all(n + 1),
        out_specs=spec_all(2),
        scratch_shapes=[pltpu.VMEM((n, size, size), f32)],
        compiler_params=pltpu.CompilerParams(vmem_limit_bytes=VMEM_BYTES),
        cost_estimate=pl.CostEstimate(
            flops=0, bytes_accessed=0, transcendentals=0
        ),
        name="weights",
    )(where, offsets, jnp.asarray(cosine_table()), head, *greens)


def product(rows_ref, first, count, left):
    right = jnp.concatenate([rows_ref[first + i] for i in range(count)], 1)
    return mm_nt(jnp.concatenate(left, 1), right)


def center_kernel(scale, group, rows_ref, weight_ref, out_ref, low_ref):
    mus, rows, width = rows_ref.shape
    total = None
    for first in range(0, mus, group):
        lines = rows_ref[first : first + group].reshape(group * rows, width)
        turned = mm(lines, weight_ref[...]).astype(bf16)
        left = [turned[i * rows : (i + 1) * rows] for i in range(group)]
        part = product(rows_ref, first, group, left)
        total = part if total is None else total + part
    out_ref[...] = scale * total
    low_ref[...] = (scale * total).astype(bf16)


def center_block(scale, turned_rows, weight, group):
    mus, rows, width = turned_rows.shape
    return pl.pallas_call(
        functools.partial(center_kernel, scale, group),
        out_shape=[
            jax.ShapeDtypeStruct((rows, rows), f32),
            jax.ShapeDtypeStruct((rows, rows), bf16),
        ],
        in_specs=spec_all(2),
        out_specs=spec_all(2),
        compiler_params=pltpu.CompilerParams(vmem_limit_bytes=VMEM_BYTES),
        cost_estimate=pl.CostEstimate(
            flops=0,
            bytes_accessed=0,
            transcendentals=0,
        ),
        name="center",
    )(turned_rows, weight)


def right_kernel(n, kb, lead, first, last, group, scale, *refs):
    far_ref, weight_ref, rows_ref = refs[:3]
    refs = refs[3:]
    total = None
    if first > 0:
        total, refs = refs[0][...], refs[1:]
    outs, flat = refs[:-1], refs[-1]
    mus, cols, width = flat.shape
    nu = far_ref.shape[2]

    def put(line, row, value):
        k = line % kb
        flat[line // kb, row : row + TILE, k * nu : (k + 1) * nu] = value

    turn(lambda r, l: far_ref[r, l : l + TILE, :], lead, cols, mus * kb, put)
    for mu in range(0, mus, group):
        lines = flat[mu : mu + group].reshape(group * cols, width)
        turned = mm(lines, weight_ref[...]).astype(bf16)
        left = [
            jnp.concatenate(
                [
                    turned[i * cols : (i + 1) * cols, q * width : (q + 1) * width]
                    for q in range(n)
                ],
                0,
            )
            for i in range(group)
        ]
        part = product(rows_ref, first + mu, group, left)
        total = part if total is None else total + part
    if last:
        for q in range(n):
            outs[q][...] = (scale * total[q * cols : (q + 1) * cols]).astype(bf16)
    else:
        outs[0][...] = total


def right_part(scale, far, lead, kb, weight, turned_rows, before, first, last, group):
    cols, lines, nu = far.shape
    cols -= lead
    mus = lines // kb
    _, rows, width = turned_rows.shape
    n = weight.shape[1] // width
    operands = [far, weight, turned_rows]
    if first > 0:
        operands.append(before)
    if last:
        out_shape = [jax.ShapeDtypeStruct((cols, rows), bf16)] * n
    else:
        out_shape = [jax.ShapeDtypeStruct((n * cols, rows), f32)]
    return pl.pallas_call(
        functools.partial(right_kernel, n, kb, lead, first, last, group, scale),
        out_shape=out_shape,
        in_specs=spec_all(len(operands)),
        out_specs=spec_all(len(out_shape)),
        scratch_shapes=[pltpu.VMEM((mus, cols, width), bf16)],
        compiler_params=pltpu.CompilerParams(vmem_limit_bytes=VMEM_BYTES),
        cost_estimate=pl.CostEstimate(
            flops=0,
            bytes_accessed=0,
            transcendentals=0,
        ),
        name="right",
    )(*operands)


def split(value):
    high = value.astype(bf16)
    return high, (value - high.astype(f32)).astype(bf16)


def screen_kernel(n, where, pattern, center_ref, below_ref, above_ref, left_ref, *refs):
    pieces, (out_ref, left, right_t) = refs[:n], refs[n:]
    me = where[0]
    cols = pieces[0].shape[0]
    size = center_ref.shape[0]
    for i in range(n):
        start = pl.multiple_of((me ^ i) * cols, cols)
        left[pl.ds(start, cols), :] = left_ref[i]
        right_t[pl.ds(start, cols), :] = pieces[i][...]
    masks = [pattern[0, e].astype(f32) for e in range(3)]
    lower = left[...] * masks[0].astype(bf16)
    upper = right_t[...].T * masks[2].astype(bf16)
    center = center_ref[...]
    high, low = split(center)
    out_ref[0, :, :size] = masks[0] * (
        lower.astype(f32) + mm(lower, below_ref[...]) + mm(high, lower) + mm(low, lower)
    )
    out_ref[0, :, size : 2 * size] = masks[1] * (
        center
        + mm_nt(lower, lower)
        + mm_nt(upper, upper)
        + mm(high, high)
        + mm(high, low)
        + mm(low, high)
    )
    out_ref[0, :, 2 * size :] = masks[2] * (
        upper.astype(f32) + mm(upper, above_ref[...]) + mm(high, upper) + mm(low, upper)
    )


def screen(where, pattern, center, below, above, left, pieces):
    n = len(pieces)
    size = center.shape[0]
    return pl.pallas_call(
        functools.partial(screen_kernel, n),
        out_shape=jax.ShapeDtypeStruct((1, size, 3 * size), f32),
        in_specs=[SMEM, SMEM] + spec_all(4 + n),
        out_specs=pl.BlockSpec(memory_space=pltpu.VMEM),
        scratch_shapes=[pltpu.VMEM((size, size), bf16)] * 2,
        compiler_params=pltpu.CompilerParams(vmem_limit_bytes=VMEM_BYTES),
        cost_estimate=pl.CostEstimate(
            flops=0, bytes_accessed=0, transcendentals=0
        ),
        name="screen",
    )(where, pattern, center, below, above, left, *pieces)


def local(tensor, g_occ, g_virt, offsets, pattern):
    rows, mus, kb, nu = tensor.shape
    lam = g_occ.shape[2]
    n = lax.axis_size("tm")
    assert n & (n - 1) == 0 and rows % n == 0
    me = lax.axis_index("tm")
    scale = 1.0 / math.sqrt(2.0 * mus * lam) / (3.0 * rows) ** 0.25
    cols = rows // n
    blocks = nu // TILE
    lines = mus * kb
    first = TILE
    where = me[None].astype(jnp.int32)
    lined = tensor.reshape(rows, lines, nu)
    split_rows = lambda x: x.reshape(blocks, TILE, lam)
    head, tail, green = prepare(
        where, offsets, lined, split_rows(g_occ), split_rows(g_virt), first, n
    )
    far_head, far_tail = shift(head, -1), shift(tail, -1)

    size = 2 * nu
    below, second = shift(green, 1), shift(green, -2)
    above = far_head[: 2 * blocks]
    stack = jnp.stack([x.reshape(size, lam) for x in (below, green, above, second)], 0)
    greens = {0: stack}
    bit = n // 2
    while bit:
        for i in list(greens):
            greens[i ^ bit] = partner(greens[i], bit)
        bit //= 2
    center_weight, right_weight = weights(
        where, offsets, far_head, 2 * blocks, [greens[i] for i in range(n)]
    )

    turned_rows = relayout(lined, kb, 4)
    center, center_low = center_block(scale, turned_rows, center_weight, 4)
    center_below, center_above = shift(center_low, 1), shift(center_low, -1)

    right_weight, center = lax.optimization_barrier((right_weight, center))
    lead = 2 * blocks + 1
    begun = right_part(scale, far_head, lead, kb, right_weight, turned_rows, None, 0, False, 4)
    parts = right_part(
        scale, far_tail, 0, kb, right_weight, turned_rows, begun[0], first // kb, True, 4
    )
    pieces = [parts[0]] + [partner(parts[i], i) for i in range(1, n)]
    left = shift(jnp.stack(pieces, 0), 1)
    return screen(where, pattern, center, center_below, center_above, left, pieces)


def solution(mesh):
    return jax.shard_map(
        local,
        mesh=mesh,
        in_specs=(
            P("region", None, None, None),
            P("tm", "region", None),
            P("tm", "region", None),
            P("region", None),
            P("region", None),
        ),
        out_specs=P("tm", "region", None),
        check_vma=False,
    )
```

```python
import functools
import math

import jax
import jax.numpy as jnp
import numpy as np
from jax import lax
from jax.experimental import pallas as pl
from jax.experimental.pallas import tpu as pltpu
from jax.sharding import PartitionSpec as P

time_points = (0.1, 0.5, 1.5, 4.0)
time_weights = (0.2, 0.6, 1.2, 2.5)
omega_points = (0.2, 0.9, 2.5, 7.0)

f32, bf16 = jnp.float32, jnp.bfloat16
VMEM_BYTES = 24 * 2**20
PREPARE_BYTES = 60 * 2**20
RELAYOUT_BYTES = 46 * 2**20
TILE = 16
COST = 3


def cosine_table():
    points = np.array(time_points, np.float32)
    weights = np.array(time_weights, np.float32)
    omegas = np.array(omega_points, np.float32)
    return weights[None, :] * np.cos(omegas[:, None] * points[None, :])


def shift(block, distance):
    devices = range(lax.axis_size("region"))
    route = [(i - distance, i) for i in devices if i - distance in devices]
    return lax.ppermute(block, "region", route)


def partner(block, bit):
    return lax.ppermute(block, "tm", [(i, i ^ bit) for i in range(lax.axis_size("tm"))])


def mm(a, b):
    return jnp.dot(a, b, preferred_element_type=f32)


def mm_nt(a, b):
    return lax.dot_general(a, b, (((1,), (1,)), ((), ())), preferred_element_type=f32)


def spec_all(count):
    return [pl.BlockSpec(memory_space=pltpu.VMEM)] * count


SMEM = pl.BlockSpec(memory_space=pltpu.SMEM)
HBM = pl.BlockSpec(memory_space=pltpu.HBM)


def swap_matrix(tile):
    size = tile * tile
    to = lax.broadcasted_iota(jnp.int32, (size, size), 0)
    of = lax.broadcasted_iota(jnp.int32, (size, size), 1)
    return (of == (to % tile) * tile + to // tile).astype(f32).astype(bf16)


def turn(source, lead, rows, lines, put):
    swap = swap_matrix(TILE)
    places = [(r, c) for r in range(0, rows, TILE) for c in range(0, lines, TILE)]
    for at in range(0, len(places), 2):
        pair = places[at : at + 2]
        blocks = [
            jnp.concatenate([source(lead + r + i, c) for i in range(TILE)], 0) for r, c in pair
        ]
        width = blocks[0].shape[1]
        moved = mm(swap, jnp.concatenate(blocks, 1)).astype(bf16)
        for h, (r, c) in enumerate(pair):
            for i in range(TILE):
                put(c + i, r, moved[i * TILE : (i + 1) * TILE, h * width : (h + 1) * width])


def relayout_kernel(kb, chunks, x_ref, out_ref, buffer, sems):
    rows, lines, nu = x_ref.shape
    part = rows // chunks
    copies = [
        pltpu.make_async_copy(
            x_ref.at[pl.ds(c * part, part)], buffer.at[pl.ds(c * part, part)], sems.at[c]
        )
        for c in range(chunks)
    ]
    for copy in copies:
        copy.start()
    for c in range(chunks):
        copies[c].wait()

        def put(line, row, value):
            k = line % kb
            start = c * part + row
            out_ref[line // kb, start : start + TILE, k * nu : (k + 1) * nu] = value

        turn(lambda r, l: buffer[r, l : l + TILE, :], c * part, part, lines, put)


def relayout(lined, kb, chunks):
    rows, lines, nu = lined.shape
    return pl.pallas_call(
        functools.partial(relayout_kernel, kb, chunks),
        out_shape=jax.ShapeDtypeStruct((lines // kb, rows, kb * nu), bf16),
        in_specs=[HBM],
        out_specs=pl.BlockSpec(memory_space=pltpu.VMEM),
        scratch_shapes=[
            pltpu.VMEM((rows, lines, nu), bf16),
            pltpu.SemaphoreType.DMA((chunks,)),
        ],
        compiler_params=pltpu.CompilerParams(vmem_limit_bytes=RELAYOUT_BYTES),
        cost_estimate=pl.CostEstimate(flops=0, bytes_accessed=4 * lined.size // COST, transcendentals=0),
        name="relayout",
    )(lined)


def prepare_kernel(first, where, offsets_ref, x_ref, occ_ref, virt_ref, head_ref, tail_ref, green_ref, offsets, sems):
    cols = tail_ref.shape[0]
    notes = head_ref.shape[0] - cols
    blocks = occ_ref.shape[0]
    lines = x_ref.shape[1]
    rows = pl.ds(where[0] * cols, cols)
    moves = [
        (offsets_ref, offsets),
        (x_ref.at[rows, pl.ds(0, first)], head_ref.at[pl.ds(notes, cols)]),
        (x_ref.at[rows, pl.ds(first, lines - first)], tail_ref),
    ]
    for ref in (head_ref, green_ref):
        moves.append((occ_ref, ref.at[pl.ds(0, blocks)]))
        moves.append((virt_ref, ref.at[pl.ds(blocks, blocks)]))
    copies = [pltpu.make_async_copy(*move, sems.at[i]) for i, move in enumerate(moves)]
    for copy in copies:
        copy.start()
    copies[0].wait()
    shape = head_ref.shape[1:]
    line = lax.broadcasted_iota(jnp.int32, shape, 0)
    values = jnp.where(line < shape[0] // 2, offsets[0, 0], offsets[0, 1])
    head_ref[2 * blocks] = values.astype(f32).astype(bf16)
    for copy in copies[1:]:
        copy.wait()


def prepare(where, offsets, lined, occ, virt, first, n):
    rows, lines, nu = lined.shape
    blocks = occ.shape[0]
    cols = rows // n
    return pl.pallas_call(
        functools.partial(prepare_kernel, first),
        out_shape=[
            jax.ShapeDtypeStruct((2 * blocks + 1 + cols, first, nu), bf16),
            jax.ShapeDtypeStruct((cols, lines - first, nu), bf16),
            jax.ShapeDtypeStruct((2 * blocks, TILE, nu), bf16),
        ],
        in_specs=[SMEM] + [HBM] * 4,
        out_specs=spec_all(3),
        scratch_shapes=[pltpu.SMEM(offsets.shape, jnp.int32), pltpu.SemaphoreType.DMA((7,))],
        compiler_params=pltpu.CompilerParams(vmem_limit_bytes=PREPARE_BYTES),
        cost_estimate=pl.CostEstimate(flops=0, bytes_accessed=4 * lined.size // n // COST, transcendentals=0),
        name="prepare",
    )(where, offsets, lined, occ, virt)


def weights_kernel(n, place, where, offsets, table, head_ref, *refs):
    greens, (center_ref, right_ref, terms) = refs[:n], refs[n:]
    nu = greens[0].shape[1] // 2
    me = where[0]
    note = head_ref[place].astype(f32)
    half = note.shape[0] // 2
    told = [jnp.max(note[:half]), jnp.max(note[half:])]
    own = [offsets[0, s] + 1 for s in range(2)]
    following = [told[s].astype(jnp.int32) + 2 for s in range(2)]

    def pick(green, places):
        occ = jnp.concatenate([green[p, :nu, :] for p in places], 0)
        virt = jnp.concatenate([green[p, nu:, :] for p in places], 0)
        return jnp.concatenate([occ, virt], 1), jnp.concatenate([virt, occ], 1)

    center = None
    for i in range(n):
        first, first_swapped = pick(greens[i], own)
        _, second_swapped = pick(greens[i], following)
        term = table[me, me ^ i] * mm_nt(first, first_swapped)
        center = term if center is None else center + term
        terms[i] = mm_nt(second_swapped, first)
    center_ref[...] = center.astype(bf16)
    size = center_ref.shape[0]
    for q in range(n):
        total = table[me ^ q, me] * terms[0]
        for i in range(1, n):
            total = total + table[me ^ q, me ^ i] * terms[i]
        right_ref[:, q * size : (q + 1) * size] = total.astype(bf16)


def weights(where, offsets, head, place, greens):
    n = len(greens)
    size = 2 * greens[0].shape[1] // 2
    return pl.pallas_call(
        functools.partial(weights_kernel, n, place),
        out_shape=[
            jax.ShapeDtypeStruct((size, size), bf16),
            jax.ShapeDtypeStruct((size, n * size), bf16),
        ],
        in_specs=[SMEM, SMEM, SMEM] + spec_all(n + 1),
        out_specs=spec_all(2),
        scratch_shapes=[pltpu.VMEM((n, size, size), f32)],
        compiler_params=pltpu.CompilerParams(vmem_limit_bytes=VMEM_BYTES),
        cost_estimate=pl.CostEstimate(
            flops=4 * n * size**3 // COST, bytes_accessed=n * size**2 * 4 // COST, transcendentals=0
        ),
        name="weights",
    )(where, offsets, jnp.asarray(cosine_table()), head, *greens)


def product(rows_ref, first, count, left):
    right = jnp.concatenate([rows_ref[first + i] for i in range(count)], 1)
    return mm_nt(jnp.concatenate(left, 1), right)


def center_kernel(scale, group, rows_ref, weight_ref, out_ref, low_ref):
    mus, rows, width = rows_ref.shape
    total = None
    for first in range(0, mus, group):
        lines = rows_ref[first : first + group].reshape(group * rows, width)
        turned = mm(lines, weight_ref[...]).astype(bf16)
        left = [turned[i * rows : (i + 1) * rows] for i in range(group)]
        part = product(rows_ref, first, group, left)
        total = part if total is None else total + part
    out_ref[...] = scale * total
    low_ref[...] = (scale * total).astype(bf16)


def center_block(scale, turned_rows, weight, group):
    mus, rows, width = turned_rows.shape
    return pl.pallas_call(
        functools.partial(center_kernel, scale, group),
        out_shape=[
            jax.ShapeDtypeStruct((rows, rows), f32),
            jax.ShapeDtypeStruct((rows, rows), bf16),
        ],
        in_specs=spec_all(2),
        out_specs=spec_all(2),
        compiler_params=pltpu.CompilerParams(vmem_limit_bytes=VMEM_BYTES),
        cost_estimate=pl.CostEstimate(
            flops=2 * mus * rows * width * (width + rows) // COST,
            bytes_accessed=2 * mus * rows * width // COST,
            transcendentals=0,
        ),
        name="center",
    )(turned_rows, weight)


def right_kernel(n, kb, lead, first, last, group, scale, *refs):
    far_ref, weight_ref, rows_ref = refs[:3]
    refs = refs[3:]
    total = None
    if first > 0:
        total, refs = refs[0][...], refs[1:]
    outs, flat = refs[:-1], refs[-1]
    mus, cols, width = flat.shape
    nu = far_ref.shape[2]

    def put(line, row, value):
        k = line % kb
        flat[line // kb, row : row + TILE, k * nu : (k + 1) * nu] = value

    turn(lambda r, l: far_ref[r, l : l + TILE, :], lead, cols, mus * kb, put)
    for mu in range(0, mus, group):
        lines = flat[mu : mu + group].reshape(group * cols, width)
        turned = mm(lines, weight_ref[...]).astype(bf16)
        left = [
            jnp.concatenate(
                [
                    turned[i * cols : (i + 1) * cols, q * width : (q + 1) * width]
                    for q in range(n)
                ],
                0,
            )
            for i in range(group)
        ]
        part = product(rows_ref, first + mu, group, left)
        total = part if total is None else total + part
    if last:
        for q in range(n):
            outs[q][...] = (scale * total[q * cols : (q + 1) * cols]).astype(bf16)
    else:
        outs[0][...] = total


def right_part(scale, far, lead, kb, weight, turned_rows, before, first, last, group):
    cols, lines, nu = far.shape
    cols -= lead
    mus = lines // kb
    _, rows, width = turned_rows.shape
    n = weight.shape[1] // width
    operands = [far, weight, turned_rows]
    if first > 0:
        operands.append(before)
    if last:
        out_shape = [jax.ShapeDtypeStruct((cols, rows), bf16)] * n
    else:
        out_shape = [jax.ShapeDtypeStruct((n * cols, rows), f32)]
    return pl.pallas_call(
        functools.partial(right_kernel, n, kb, lead, first, last, group, scale),
        out_shape=out_shape,
        in_specs=spec_all(len(operands)),
        out_specs=spec_all(len(out_shape)),
        scratch_shapes=[pltpu.VMEM((mus, cols, width), bf16)],
        compiler_params=pltpu.CompilerParams(vmem_limit_bytes=VMEM_BYTES),
        cost_estimate=pl.CostEstimate(
            flops=2 * mus * cols * n * width * (width + rows) // COST,
            bytes_accessed=2 * mus * rows * width // COST,
            transcendentals=0,
        ),
        name="right",
    )(*operands)


def split(value):
    high = value.astype(bf16)
    return high, (value - high.astype(f32)).astype(bf16)


def upper_kernel(n, where, pattern, center_ref, above_ref, *refs):
    pieces, (out_ref, middle_ref, right_t, block, sem) = refs[:n], refs[n:]
    me = where[0]
    cols = pieces[0].shape[0]
    size = center_ref.shape[0]
    for i in range(n):
        start = pl.multiple_of((me ^ i) * cols, cols)
        right_t[pl.ds(start, cols), :] = pieces[i][...]
    mask = pattern[0, 2].astype(f32)
    upper = right_t[...].T * mask.astype(bf16)
    center = center_ref[...]
    high, low = split(center)
    block[...] = mask * (
        upper.astype(f32) + mm(upper, above_ref[...]) + mm(high, upper) + mm(low, upper)
    )
    copy = pltpu.make_async_copy(block, out_ref.at[0, :, pl.ds(2 * size, size)], sem)
    copy.start()
    middle_ref[...] = (
        center + mm_nt(upper, upper) + mm(high, high) + mm(high, low) + mm(low, high)
    )
    copy.wait()


def upper_blocks(where, pattern, center, above, pieces):
    n = len(pieces)
    size = center.shape[0]
    return pl.pallas_call(
        functools.partial(upper_kernel, n),
        out_shape=[
            jax.ShapeDtypeStruct((1, size, 3 * size), f32),
            jax.ShapeDtypeStruct((size, size), f32),
        ],
        in_specs=[SMEM, SMEM] + spec_all(2 + n),
        out_specs=[HBM] + spec_all(1),
        scratch_shapes=[
            pltpu.VMEM((size, size), bf16),
            pltpu.VMEM((size, size), f32),
            pltpu.SemaphoreType.DMA,
        ],
        compiler_params=pltpu.CompilerParams(vmem_limit_bytes=VMEM_BYTES),
        cost_estimate=pl.CostEstimate(
            flops=16 * size**3 // COST, bytes_accessed=12 * size**2 // COST, transcendentals=0
        ),
        name="upper",
    )(where, pattern, center, above, *pieces)


def lower_kernel(n, where, pattern, center_ref, middle_ref, below_ref, left_ref, _, out_ref, left, blocks, sems):
    me = where[0]
    cols = left_ref.shape[1]
    size = center_ref.shape[0]
    for i in range(n):
        start = pl.multiple_of((me ^ i) * cols, cols)
        left[pl.ds(start, cols), :] = left_ref[i]
    masks = [pattern[0, e].astype(f32) for e in range(2)]
    lower = left[...] * masks[0].astype(bf16)
    high, low = split(center_ref[...])
    copies = [
        pltpu.make_async_copy(
            blocks.at[e], out_ref.at[0, :, pl.ds(e * size, size)], sems.at[e]
        )
        for e in range(2)
    ]
    blocks[0] = masks[0] * (
        lower.astype(f32) + mm(lower, below_ref[...]) + mm(high, lower) + mm(low, lower)
    )
    copies[0].start()
    blocks[1] = masks[1] * (middle_ref[...] + mm_nt(lower, lower))
    copies[1].start()
    for copy in copies:
        copy.wait()


def lower_blocks(where, pattern, center, middle, below, left, out):
    n = left.shape[0]
    size = center.shape[0]
    return pl.pallas_call(
        functools.partial(lower_kernel, n),
        out_shape=jax.ShapeDtypeStruct((1, size, 3 * size), f32),
        in_specs=[SMEM, SMEM] + spec_all(4) + [HBM],
        out_specs=HBM,
        input_output_aliases={6: 0},
        scratch_shapes=[
            pltpu.VMEM((size, size), bf16),
            pltpu.VMEM((2, size, size), f32),
            pltpu.SemaphoreType.DMA((2,)),
        ],
        compiler_params=pltpu.CompilerParams(vmem_limit_bytes=VMEM_BYTES),
        cost_estimate=pl.CostEstimate(
            flops=10 * size**3 // COST, bytes_accessed=12 * size**2 // COST, transcendentals=0
        ),
        name="lower",
    )(where, pattern, center, middle, below, left, out)


def local(tensor, g_occ, g_virt, offsets, pattern):
    rows, mus, kb, nu = tensor.shape
    lam = g_occ.shape[2]
    n = lax.axis_size("tm")
    assert n & (n - 1) == 0 and rows % n == 0
    me = lax.axis_index("tm")
    scale = 1.0 / math.sqrt(2.0 * mus * lam) / (3.0 * rows) ** 0.25
    cols = rows // n
    blocks = nu // TILE
    lines = mus * kb
    first = TILE
    where = me[None].astype(jnp.int32)
    lined = tensor.reshape(rows, lines, nu)
    split_rows = lambda x: x.reshape(blocks, TILE, lam)
    head, tail, green = prepare(
        where, offsets, lined, split_rows(g_occ), split_rows(g_virt), first, n
    )
    far_head, far_tail = shift(head, -1), shift(tail, -1)

    size = 2 * nu
    below, second = shift(green, 1), shift(green, -2)
    above = far_head[: 2 * blocks]
    stack = jnp.stack([x.reshape(size, lam) for x in (below, green, above, second)], 0)
    turned_rows = relayout(lined, kb, 4)
    stack, turned_rows = lax.optimization_barrier((stack, turned_rows))
    greens = {0: stack}
    bit = n // 2
    while bit:
        for i in list(greens):
            greens[i ^ bit] = partner(greens[i], bit)
        bit //= 2
    center_weight, right_weight = weights(
        where, offsets, far_head, 2 * blocks, [greens[i] for i in range(n)]
    )

    center, center_low = center_block(scale, turned_rows, center_weight, 4)

    right_weight, center = lax.optimization_barrier((right_weight, center))
    lead = 2 * blocks + 1
    begun = right_part(scale, far_head, lead, kb, right_weight, turned_rows, None, 0, False, 4)
    parts = right_part(
        scale, far_tail, 0, kb, right_weight, turned_rows, begun[0], first // kb, True, 4
    )
    pieces = [parts[0]] + [partner(parts[i], i) for i in range(1, n)]
    center_below, center_above = shift(center_low, 1), shift(center_low, -1)
    *pieces, center_below, center_above = lax.optimization_barrier(
        (*pieces, center_below, center_above)
    )
    left = shift(jnp.stack(pieces, 0), 1)
    out, middle = upper_blocks(where, pattern, center, center_above, pieces)
    return lower_blocks(where, pattern, center, middle, center_below, left, out)


def solution(mesh):
    return jax.shard_map(
        local,
        mesh=mesh,
        in_specs=(
            P("region", None, None, None),
            P("tm", "region", None),
            P("tm", "region", None),
            P("region", None),
            P("region", None),
        ),
        out_specs=P("tm", "region", None),
        check_vma=False,
    )
```

```python
import functools
import math

import jax
import jax.numpy as jnp
import numpy as np
from jax import lax
from jax.experimental import pallas as pl
from jax.experimental.pallas import tpu as pltpu
from jax.sharding import PartitionSpec as P

time_points = (0.1, 0.5, 1.5, 4.0)
time_weights = (0.2, 0.6, 1.2, 2.5)
omega_points = (0.2, 0.9, 2.5, 7.0)

f32, bf16 = jnp.float32, jnp.bfloat16
VMEM_BYTES = 24 * 2**20
PREPARE_BYTES = 59 * 2**20
RELAYOUT_BYTES = 46 * 2**20
TILE = 16
COST = 3


def cosine_table():
    points = np.array(time_points, np.float32)
    weights = np.array(time_weights, np.float32)
    omegas = np.array(omega_points, np.float32)
    return weights[None, :] * np.cos(omegas[:, None] * points[None, :])


def shift(block, distance):
    devices = range(lax.axis_size("region"))
    route = [(i - distance, i) for i in devices if i - distance in devices]
    return lax.ppermute(block, "region", route)


def partner(block, bit):
    return lax.ppermute(block, "tm", [(i, i ^ bit) for i in range(lax.axis_size("tm"))])


def mm(a, b):
    return jnp.dot(a, b, preferred_element_type=f32)


def mm_nt(a, b):
    return lax.dot_general(a, b, (((1,), (1,)), ((), ())), preferred_element_type=f32)


def spec_all(count):
    return [pl.BlockSpec(memory_space=pltpu.VMEM)] * count


SMEM = pl.BlockSpec(memory_space=pltpu.SMEM)
HBM = pl.BlockSpec(memory_space=pltpu.HBM)


def swap_matrix(tile):
    size = tile * tile
    to = lax.broadcasted_iota(jnp.int32, (size, size), 0)
    of = lax.broadcasted_iota(jnp.int32, (size, size), 1)
    return (of == (to % tile) * tile + to // tile).astype(f32).astype(bf16)


def turn(source, lead, rows, lines, put):
    swap = swap_matrix(TILE)
    places = [(r, c) for r in range(0, rows, TILE) for c in range(0, lines, TILE)]
    for at in range(0, len(places), 2):
        pair = places[at : at + 2]
        blocks = [
            jnp.concatenate([source(lead + r + i, c) for i in range(TILE)], 0) for r, c in pair
        ]
        width = blocks[0].shape[1]
        moved = mm(swap, jnp.concatenate(blocks, 1)).astype(bf16)
        for h, (r, c) in enumerate(pair):
            for i in range(TILE):
                put(c + i, r, moved[i * TILE : (i + 1) * TILE, h * width : (h + 1) * width])


def relayout_kernel(kb, chunks, x_ref, out_ref, buffer, sems):
    rows, lines, nu = x_ref.shape
    part = rows // chunks
    copies = [
        pltpu.make_async_copy(
            x_ref.at[pl.ds(c * part, part)], buffer.at[pl.ds(c * part, part)], sems.at[c]
        )
        for c in range(chunks)
    ]
    for copy in copies:
        copy.start()
    for c in range(chunks):
        copies[c].wait()

        def put(line, row, value):
            k = line % kb
            start = c * part + row
            out_ref[line // kb, start : start + TILE, k * nu : (k + 1) * nu] = value

        turn(lambda r, l: buffer[r, l : l + TILE, :], c * part, part, lines, put)


def relayout(lined, kb, chunks):
    rows, lines, nu = lined.shape
    return pl.pallas_call(
        functools.partial(relayout_kernel, kb, chunks),
        out_shape=jax.ShapeDtypeStruct((lines // kb, rows, kb * nu), bf16),
        in_specs=[HBM],
        out_specs=pl.BlockSpec(memory_space=pltpu.VMEM),
        scratch_shapes=[
            pltpu.VMEM((rows, lines, nu), bf16),
            pltpu.SemaphoreType.DMA((chunks,)),
        ],
        compiler_params=pltpu.CompilerParams(vmem_limit_bytes=RELAYOUT_BYTES),
        cost_estimate=pl.CostEstimate(flops=0, bytes_accessed=4 * lined.size // COST, transcendentals=0),
        name="relayout",
    )(lined)


def pieces_of(span, cols):
    runs, at = [], span[0]
    while at < span[1]:
        group, row = divmod(at, cols)
        count = min(cols - row, span[1] - at)
        runs.append((group, row, count, at - span[0]))
        at += count
    return runs


def prepare_kernel(spans, cols, offsets_ref, x_ref, occ_ref, virt_ref, *refs):
    parts, (offsets, sems) = refs[: len(spans)], refs[len(spans) :]
    blocks, tile, _ = occ_ref.shape
    mine = lax.axis_index("tm") * cols
    head_ref = parts[0]
    moves = [
        (offsets_ref, offsets),
        (occ_ref, head_ref.at[pl.ds(0, blocks)]),
        (virt_ref, head_ref.at[pl.ds(blocks, blocks)]),
    ]
    for ref, span in zip(parts, spans):
        lead = 2 * blocks + 1 if ref is head_ref else 0
        for group, row, count, place in pieces_of(span, cols):
            source = x_ref.at[pl.ds(mine + row, count), pl.ds(group * tile, tile)]
            moves.append((source, ref.at[pl.ds(lead + place, count)]))
    copies = [pltpu.make_async_copy(*move, sems.at[i]) for i, move in enumerate(moves)]
    for copy in copies:
        copy.start()
    copies[0].wait()
    shape = head_ref.shape[1:]
    line = lax.broadcasted_iota(jnp.int32, shape, 0)
    values = jnp.where(line < shape[0] // 2, offsets[0, 0], offsets[0, 1])
    head_ref[2 * blocks] = values.astype(f32).astype(bf16)
    for copy in copies[1:]:
        copy.wait()


def prepare(offsets, lined, occ, virt, spans, n):
    rows, _, nu = lined.shape
    blocks, tile, _ = occ.shape
    cols = rows // n
    tiles = [last - first for first, last in spans]
    tiles[0] += 2 * blocks + 1
    moves = 3 + sum(len(pieces_of(span, cols)) for span in spans)
    return pl.pallas_call(
        functools.partial(prepare_kernel, spans, cols),
        out_shape=[jax.ShapeDtypeStruct((t, tile, nu), bf16) for t in tiles],
        in_specs=[HBM] * 4,
        out_specs=spec_all(len(spans)),
        scratch_shapes=[
            pltpu.SMEM(offsets.shape, jnp.int32),
            pltpu.SemaphoreType.DMA((moves,)),
        ],
        compiler_params=pltpu.CompilerParams(vmem_limit_bytes=PREPARE_BYTES),
        cost_estimate=pl.CostEstimate(flops=0, bytes_accessed=2**20 // COST, transcendentals=0),
        name="prepare",
    )(offsets, lined, occ, virt)


def weights_kernel(n, place, offsets, table, head_ref, *refs):
    greens, (center_ref, right_ref, terms) = refs[:n], refs[n:]
    nu = greens[0].shape[1] // 2
    me = lax.axis_index("tm")
    note = head_ref[place].astype(f32)
    half = note.shape[0] // 2
    told = [jnp.max(note[:half]), jnp.max(note[half:])]
    own = [offsets[0, s] + 1 for s in range(2)]
    following = [told[s].astype(jnp.int32) + 2 for s in range(2)]

    def pick(green, places):
        occ = jnp.concatenate([green[p, :nu, :] for p in places], 0)
        virt = jnp.concatenate([green[p, nu:, :] for p in places], 0)
        return jnp.concatenate([occ, virt], 1), jnp.concatenate([virt, occ], 1)

    center = None
    for i in range(n):
        first, first_swapped = pick(greens[i], own)
        _, second_swapped = pick(greens[i], following)
        term = table[me, me ^ i] * mm_nt(first, first_swapped)
        center = term if center is None else center + term
        terms[i] = mm_nt(second_swapped, first)
    center_ref[...] = center.astype(bf16)
    size = center_ref.shape[0]
    for q in range(n):
        total = table[me ^ q, me] * terms[0]
        for i in range(1, n):
            total = total + table[me ^ q, me ^ i] * terms[i]
        right_ref[:, q * size : (q + 1) * size] = total.astype(bf16)


def weights(offsets, head, place, greens):
    n = len(greens)
    size = 2 * greens[0].shape[1] // 2
    return pl.pallas_call(
        functools.partial(weights_kernel, n, place),
        out_shape=[
            jax.ShapeDtypeStruct((size, size), bf16),
            jax.ShapeDtypeStruct((size, n * size), bf16),
        ],
        in_specs=[SMEM, SMEM] + spec_all(n + 1),
        out_specs=spec_all(2),
        scratch_shapes=[pltpu.VMEM((n, size, size), f32)],
        compiler_params=pltpu.CompilerParams(vmem_limit_bytes=VMEM_BYTES),
        cost_estimate=pl.CostEstimate(
            flops=4 * n * size**3 // COST, bytes_accessed=n * size**2 * 4 // COST, transcendentals=0
        ),
        name="weights",
    )(offsets, jnp.asarray(cosine_table()), head, *greens)


def product(rows_ref, first, count, left):
    right = jnp.concatenate([rows_ref[first + i] for i in range(count)], 1)
    return mm_nt(jnp.concatenate(left, 1), right)


def center_kernel(scale, group, rows_ref, weight_ref, out_ref, low_ref):
    mus, rows, width = rows_ref.shape
    total = None
    for first in range(0, mus, group):
        lines = rows_ref[first : first + group].reshape(group * rows, width)
        turned = mm(lines, weight_ref[...]).astype(bf16)
        left = [turned[i * rows : (i + 1) * rows] for i in range(group)]
        part = product(rows_ref, first, group, left)
        total = part if total is None else total + part
    out_ref[...] = scale * total
    low_ref[...] = (scale * total).astype(bf16)


def center_block(scale, turned_rows, weight, group):
    mus, rows, width = turned_rows.shape
    return pl.pallas_call(
        functools.partial(center_kernel, scale, group),
        out_shape=[
            jax.ShapeDtypeStruct((rows, rows), f32),
            jax.ShapeDtypeStruct((rows, rows), bf16),
        ],
        in_specs=spec_all(2),
        out_specs=spec_all(2),
        compiler_params=pltpu.CompilerParams(vmem_limit_bytes=VMEM_BYTES),
        cost_estimate=pl.CostEstimate(
            flops=2 * mus * rows * width * (width + rows) // COST,
            bytes_accessed=2 * mus * rows * width // COST,
            transcendentals=0,
        ),
        name="center",
    )(turned_rows, weight)


def right_kernel(n, kb, spans, leads, groups, first, last, group, scale, *refs):
    fars, refs = refs[: len(spans)], refs[len(spans) :]
    weight_ref, rows_ref = refs[:2]
    refs = refs[2:]
    total = None
    if not first:
        total, refs = refs[0][...], refs[1:]
    outs, flat = refs[:-1], refs[-1]
    mus, cols, width = flat.shape
    nu = width // kb
    start = groups[0] * TILE

    def source(row, line):
        at = (start + line) // TILE * cols + row
        for far, span, lead in zip(fars, spans, leads):
            if span[0] <= at < span[1]:
                return far[lead + at - span[0]]

    def put(line, row, value):
        k = line % kb
        flat[line // kb, row : row + TILE, k * nu : (k + 1) * nu] = value

    turn(source, 0, cols, mus * kb, put)
    for mu in range(0, mus, group):
        lines = flat[mu : mu + group].reshape(group * cols, width)
        turned = mm(lines, weight_ref[...]).astype(bf16)
        left = [
            jnp.concatenate(
                [
                    turned[i * cols : (i + 1) * cols, q * width : (q + 1) * width]
                    for q in range(n)
                ],
                0,
            )
            for i in range(group)
        ]
        part = product(rows_ref, start // kb + mu, group, left)
        total = part if total is None else total + part
    if last:
        for q in range(n):
            outs[q][...] = (scale * total[q * cols : (q + 1) * cols]).astype(bf16)
    else:
        outs[0][...] = total


def right_part(scale, fars, spans, leads, kb, weight, turned_rows, before, groups, last, group):
    _, rows, width = turned_rows.shape
    n = weight.shape[1] // width
    cols = rows // n
    mus = (groups[1] - groups[0]) * TILE // kb
    operands = [*fars, weight, turned_rows]
    if before is not None:
        operands.append(before)
    if last:
        out_shape = [jax.ShapeDtypeStruct((cols, rows), bf16)] * n
    else:
        out_shape = [jax.ShapeDtypeStruct((n * cols, rows), f32)]
    return pl.pallas_call(
        functools.partial(
            right_kernel, n, kb, spans, leads, groups, before is None, last, group, scale
        ),
        out_shape=out_shape,
        in_specs=spec_all(len(operands)),
        out_specs=spec_all(len(out_shape)),
        scratch_shapes=[pltpu.VMEM((mus, cols, width), bf16)],
        compiler_params=pltpu.CompilerParams(vmem_limit_bytes=VMEM_BYTES),
        cost_estimate=pl.CostEstimate(
            flops=2 * mus * cols * n * width * (width + rows) // COST,
            bytes_accessed=2 * mus * rows * width // COST,
            transcendentals=0,
        ),
        name="right",
    )(*operands)


def split(value):
    high = value.astype(bf16)
    return high, (value - high.astype(f32)).astype(bf16)


def upper_kernel(n, pattern, center_ref, above_ref, *refs):
    pieces, (out_ref, middle_ref, right_t, block, sem) = refs[:n], refs[n:]
    me = lax.axis_index("tm")
    cols = pieces[0].shape[0]
    size = center_ref.shape[0]
    for i in range(n):
        start = pl.multiple_of((me ^ i) * cols, cols)
        right_t[pl.ds(start, cols), :] = pieces[i][...]
    mask = pattern[0, 2].astype(f32)
    upper = right_t[...].T * mask.astype(bf16)
    center = center_ref[...]
    high, low = split(center)
    block[...] = mask * (
        upper.astype(f32) + mm(upper, above_ref[...]) + mm(high, upper) + mm(low, upper)
    )
    copy = pltpu.make_async_copy(block, out_ref.at[0, :, pl.ds(2 * size, size)], sem)
    copy.start()
    middle_ref[...] = (
        center + mm_nt(upper, upper) + mm(high, high) + mm(high, low) + mm(low, high)
    )
    copy.wait()


def upper_blocks(pattern, center, above, pieces):
    n = len(pieces)
    size = center.shape[0]
    return pl.pallas_call(
        functools.partial(upper_kernel, n),
        out_shape=[
            jax.ShapeDtypeStruct((1, size, 3 * size), f32),
            jax.ShapeDtypeStruct((size, size), f32),
        ],
        in_specs=[SMEM] + spec_all(2 + n),
        out_specs=[HBM] + spec_all(1),
        scratch_shapes=[
            pltpu.VMEM((size, size), bf16),
            pltpu.VMEM((size, size), f32),
            pltpu.SemaphoreType.DMA,
        ],
        compiler_params=pltpu.CompilerParams(vmem_limit_bytes=VMEM_BYTES),
        cost_estimate=pl.CostEstimate(
            flops=16 * size**3 // COST, bytes_accessed=12 * size**2 // COST, transcendentals=0
        ),
        name="upper",
    )(pattern, center, above, *pieces)


def lower_kernel(n, pattern, center_ref, middle_ref, below_ref, left_ref, _, out_ref, left, blocks, sems):
    me = lax.axis_index("tm")
    cols = left_ref.shape[1]
    size = center_ref.shape[0]
    for i in range(n):
        start = pl.multiple_of((me ^ i) * cols, cols)
        left[pl.ds(start, cols), :] = left_ref[i]
    masks = [pattern[0, e].astype(f32) for e in range(2)]
    lower = left[...] * masks[0].astype(bf16)
    high, low = split(center_ref[...])
    copies = [
        pltpu.make_async_copy(
            blocks.at[e], out_ref.at[0, :, pl.ds(e * size, size)], sems.at[e]
        )
        for e in range(2)
    ]
    blocks[0] = masks[0] * (
        lower.astype(f32) + mm(lower, below_ref[...]) + mm(high, lower) + mm(low, lower)
    )
    copies[0].start()
    blocks[1] = masks[1] * (middle_ref[...] + mm_nt(lower, lower))
    copies[1].start()
    for copy in copies:
        copy.wait()


def lower_blocks(pattern, center, middle, below, left, out):
    n = left.shape[0]
    size = center.shape[0]
    return pl.pallas_call(
        functools.partial(lower_kernel, n),
        out_shape=jax.ShapeDtypeStruct((1, size, 3 * size), f32),
        in_specs=[SMEM] + spec_all(4) + [HBM],
        out_specs=HBM,
        input_output_aliases={5: 0},
        scratch_shapes=[
            pltpu.VMEM((size, size), bf16),
            pltpu.VMEM((2, size, size), f32),
            pltpu.SemaphoreType.DMA((2,)),
        ],
        compiler_params=pltpu.CompilerParams(vmem_limit_bytes=VMEM_BYTES),
        cost_estimate=pl.CostEstimate(
            flops=10 * size**3 // COST, bytes_accessed=12 * size**2 // COST, transcendentals=0
        ),
        name="lower",
    )(pattern, center, middle, below, left, out)


def local(tensor, g_occ, g_virt, offsets, pattern):
    rows, mus, kb, nu = tensor.shape
    lam = g_occ.shape[2]
    n = lax.axis_size("tm")
    assert n & (n - 1) == 0 and rows % n == 0
    scale = 1.0 / math.sqrt(2.0 * mus * lam) / (3.0 * rows) ** 0.25
    blocks = nu // TILE
    lines = mus * kb
    groups, cols = lines // TILE, rows // n
    cuts = (0, 64, groups * cols)
    spans = tuple(zip(cuts, cuts[1:]))
    lined = tensor.reshape(rows, lines, nu)
    split_rows = lambda x: x.reshape(blocks, TILE, lam)
    own = jnp.concatenate([g_occ[0], g_virt[0]], 0)
    below, second = shift(own, 1), shift(own, -2)
    head, tail = prepare(offsets, lined, split_rows(g_occ), split_rows(g_virt), spans, n)
    far_head, far_tail = shift(head, -1), shift(tail, -1)

    size = 2 * nu
    above = far_head[: 2 * blocks]
    stack = jnp.stack([x.reshape(size, lam) for x in (below, own, above, second)], 0)
    turned_rows = relayout(lined, kb, 4)
    greens = {0: stack}
    bit = n // 2
    while bit:
        for i in list(greens):
            if i:
                greens[i], turned_rows = lax.optimization_barrier((greens[i], turned_rows))
            greens[i ^ bit] = partner(greens[i], bit)
        bit //= 2
    center_weight, right_weight = weights(
        offsets, far_head, 2 * blocks, [greens[i] for i in range(n)]
    )

    center, center_low = center_block(scale, turned_rows, center_weight, 4)

    right_weight, center = lax.optimization_barrier((right_weight, center))
    lead = 2 * blocks + 1
    parts = right_part(
        scale, (far_head, far_tail), spans, (lead, 0), kb, right_weight, turned_rows,
        None, (0, groups), True, 4,
    )
    pieces = [parts[0]] + [partner(parts[i], i) for i in range(1, n)]
    center_below, center_above = shift(center_low, 1), shift(center_low, -1)
    *pieces, center_above = lax.optimization_barrier((*pieces, center_above))
    left = shift(jnp.stack(pieces, 0), 1)
    out, middle = upper_blocks(pattern, center, center_above, pieces)
    return lower_blocks(pattern, center, middle, center_below, left, out)


def solution(mesh):
    return jax.shard_map(
        local,
        mesh=mesh,
        in_specs=(
            P("region", None, None, None),
            P("tm", "region", None),
            P("tm", "region", None),
            P("region", None),
            P("region", None),
        ),
        out_specs=P("tm", "region", None),
        check_vma=False,
    )
```

```python
import functools
import math

import jax
import jax.numpy as jnp
import numpy as np
from jax import lax
from jax.experimental import pallas as pl
from jax.experimental.pallas import tpu as pltpu
from jax.sharding import PartitionSpec as P

time_points = (0.1, 0.5, 1.5, 4.0)
time_weights = (0.2, 0.6, 1.2, 2.5)
omega_points = (0.2, 0.9, 2.5, 7.0)

f32, bf16 = jnp.float32, jnp.bfloat16
VMEM_BYTES = 24 * 2**20
PREPARE_BYTES = 59 * 2**20
RELAYOUT_BYTES = 46 * 2**20
TILE = 16
COST = 3


def cosine_table():
    points = np.array(time_points, np.float32)
    weights = np.array(time_weights, np.float32)
    omegas = np.array(omega_points, np.float32)
    return weights[None, :] * np.cos(omegas[:, None] * points[None, :])


def shift(block, distance):
    devices = range(lax.axis_size("region"))
    route = [(i - distance, i) for i in devices if i - distance in devices]
    return lax.ppermute(block, "region", route)


def swap_pairs(block, first):
    count = lax.axis_size("region")
    route = []
    for i in range(first, count - 1, 2):
        route += [(i, i + 1), (i + 1, i)]
    return lax.ppermute(block, "region", route)


def partner(block, bit):
    return lax.ppermute(block, "tm", [(i, i ^ bit) for i in range(lax.axis_size("tm"))])


def mm(a, b):
    return jnp.dot(a, b, preferred_element_type=f32)


def mm_nt(a, b):
    return lax.dot_general(a, b, (((1,), (1,)), ((), ())), preferred_element_type=f32)


def spec_all(count):
    return [pl.BlockSpec(memory_space=pltpu.VMEM)] * count


SMEM = pl.BlockSpec(memory_space=pltpu.SMEM)
HBM = pl.BlockSpec(memory_space=pltpu.HBM)


def swap_matrix(tile):
    size = tile * tile
    to = lax.broadcasted_iota(jnp.int32, (size, size), 0)
    of = lax.broadcasted_iota(jnp.int32, (size, size), 1)
    return (of == (to % tile) * tile + to // tile).astype(f32).astype(bf16)


def turn(source, lead, rows, lines, put):
    swap = swap_matrix(TILE)
    places = [(r, c) for r in range(0, rows, TILE) for c in range(0, lines, TILE)]
    for at in range(0, len(places), 2):
        pair = places[at : at + 2]
        blocks = [
            jnp.concatenate([source(lead + r + i, c) for i in range(TILE)], 0) for r, c in pair
        ]
        width = blocks[0].shape[1]
        moved = mm(swap, jnp.concatenate(blocks, 1)).astype(bf16)
        for h, (r, c) in enumerate(pair):
            for i in range(TILE):
                put(c + i, r, moved[i * TILE : (i + 1) * TILE, h * width : (h + 1) * width])


def relayout_kernel(kb, chunks, x_ref, out_ref, buffer, sems):
    rows, lines, nu = x_ref.shape
    part = rows // chunks
    copies = [
        pltpu.make_async_copy(
            x_ref.at[pl.ds(c * part, part)], buffer.at[pl.ds(c * part, part)], sems.at[c]
        )
        for c in range(chunks)
    ]
    for copy in copies:
        copy.start()
    for c in range(chunks):
        copies[c].wait()

        def put(line, row, value):
            k = line % kb
            start = c * part + row
            out_ref[line // kb, start : start + TILE, k * nu : (k + 1) * nu] = value

        turn(lambda r, l: buffer[r, l : l + TILE, :], c * part, part, lines, put)


def relayout(lined, kb, chunks):
    rows, lines, nu = lined.shape
    return pl.pallas_call(
        functools.partial(relayout_kernel, kb, chunks),
        out_shape=jax.ShapeDtypeStruct((lines // kb, rows, kb * nu), bf16),
        in_specs=[HBM],
        out_specs=pl.BlockSpec(memory_space=pltpu.VMEM),
        scratch_shapes=[
            pltpu.VMEM((rows, lines, nu), bf16),
            pltpu.SemaphoreType.DMA((chunks,)),
        ],
        compiler_params=pltpu.CompilerParams(vmem_limit_bytes=RELAYOUT_BYTES),
        cost_estimate=pl.CostEstimate(flops=0, bytes_accessed=4 * lined.size // COST, transcendentals=0),
        name="relayout",
    )(lined)


def pieces_of(span, cols):
    runs, at = [], span[0]
    while at < span[1]:
        group, row = divmod(at, cols)
        count = min(cols - row, span[1] - at)
        runs.append((group, row, count, at - span[0]))
        at += count
    return runs


def prepare_kernel(spans, cols, offsets_ref, x_ref, occ_ref, virt_ref, *refs):
    parts, (note_ref, offsets, sems) = refs[: len(spans)], refs[len(spans) :]
    blocks, tile, _ = occ_ref.shape
    mine = lax.axis_index("tm") * cols
    head_ref = parts[0]
    moves = [
        (offsets_ref, offsets),
        (occ_ref, head_ref.at[pl.ds(0, blocks)]),
        (virt_ref, head_ref.at[pl.ds(blocks, blocks)]),
    ]
    for ref, span in zip(parts, spans):
        lead = 2 * blocks + 1 if ref is head_ref else 0
        for group, row, count, place in pieces_of(span, cols):
            source = x_ref.at[pl.ds(mine + row, count), pl.ds(group * tile, tile)]
            moves.append((source, ref.at[pl.ds(lead + place, count)]))
    copies = [pltpu.make_async_copy(*move, sems.at[i]) for i, move in enumerate(moves)]
    for copy in copies:
        copy.start()
    copies[0].wait()
    shape = head_ref.shape[1:]
    line = lax.broadcasted_iota(jnp.int32, shape, 0)
    values = jnp.where(line < shape[0] // 2, offsets[0, 0], offsets[0, 1])
    note_ref[...] = values.astype(f32).astype(bf16)
    head_ref[2 * blocks] = note_ref[...]
    for copy in copies[1:]:
        copy.wait()


def prepare(offsets, lined, occ, virt, spans, n):
    rows, _, nu = lined.shape
    blocks, tile, _ = occ.shape
    cols = rows // n
    tiles = [last - first for first, last in spans]
    tiles[0] += 2 * blocks + 1
    moves = 3 + sum(len(pieces_of(span, cols)) for span in spans)
    return pl.pallas_call(
        functools.partial(prepare_kernel, spans, cols),
        out_shape=[jax.ShapeDtypeStruct((t, tile, nu), bf16) for t in tiles]
        + [jax.ShapeDtypeStruct((tile, nu), bf16)],
        in_specs=[HBM] * 4,
        out_specs=spec_all(len(spans) + 1),
        scratch_shapes=[
            pltpu.SMEM(offsets.shape, jnp.int32),
            pltpu.SemaphoreType.DMA((moves,)),
        ],
        compiler_params=pltpu.CompilerParams(vmem_limit_bytes=PREPARE_BYTES),
        cost_estimate=pl.CostEstimate(flops=0, bytes_accessed=2**20 // COST, transcendentals=0),
        name="prepare",
    )(offsets, lined, occ, virt)


def weights_kernel(n, place, note_ref, head_ref, *refs):
    greens, (center_ref, right_ref, terms) = refs[:n], refs[n:]
    nu = greens[0].shape[1] // 2
    me = lax.axis_index("tm")
    table = cosine_table()

    def weight(frequency, time):
        value = jnp.float32(table[frequency, time])
        for m in range(1, n):
            value = jnp.where(me == m, jnp.float32(table[m ^ frequency, m ^ time]), value)
        return value

    def told(note):
        note = note.astype(f32)
        half = note.shape[0] // 2
        return [jnp.max(note[:half]).astype(jnp.int32), jnp.max(note[half:]).astype(jnp.int32)]

    own = [offset + 1 for offset in told(note_ref[...])]
    following = [offset + 2 for offset in told(head_ref[place])]

    def pick(green, places):
        occ = jnp.concatenate([green[p, :nu, :] for p in places], 0)
        virt = jnp.concatenate([green[p, nu:, :] for p in places], 0)
        return jnp.concatenate([occ, virt], 1), jnp.concatenate([virt, occ], 1)

    center = None
    for i in range(n):
        first, first_swapped = pick(greens[i], own)
        _, second_swapped = pick(greens[i], following)
        term = weight(0, i) * mm_nt(first, first_swapped)
        center = term if center is None else center + term
        terms[i] = mm_nt(second_swapped, first)
    center_ref[...] = center.astype(bf16)
    size = center_ref.shape[0]
    for q in range(n):
        total = weight(q, 0) * terms[0]
        for i in range(1, n):
            total = total + weight(q, i) * terms[i]
        right_ref[:, q * size : (q + 1) * size] = total.astype(bf16)


def weights(note, head, place, greens):
    n = len(greens)
    size = 2 * greens[0].shape[1] // 2
    return pl.pallas_call(
        functools.partial(weights_kernel, n, place),
        out_shape=[
            jax.ShapeDtypeStruct((size, size), bf16),
            jax.ShapeDtypeStruct((size, n * size), bf16),
        ],
        in_specs=spec_all(n + 2),
        out_specs=spec_all(2),
        scratch_shapes=[pltpu.VMEM((n, size, size), f32)],
        compiler_params=pltpu.CompilerParams(vmem_limit_bytes=VMEM_BYTES),
        cost_estimate=pl.CostEstimate(
            flops=4 * n * size**3 // COST, bytes_accessed=n * size**2 * 4 // COST, transcendentals=0
        ),
        name="weights",
    )(note, head, *greens)


def product(rows_ref, first, count, left):
    right = jnp.concatenate([rows_ref[first + i] for i in range(count)], 1)
    return mm_nt(jnp.concatenate(left, 1), right)


def center_kernel(scale, group, rows_ref, weight_ref, out_ref, low_ref):
    mus, rows, width = rows_ref.shape
    total = None
    for first in range(0, mus, group):
        lines = rows_ref[first : first + group].reshape(group * rows, width)
        turned = mm(lines, weight_ref[...]).astype(bf16)
        left = [turned[i * rows : (i + 1) * rows] for i in range(group)]
        part = product(rows_ref, first, group, left)
        total = part if total is None else total + part
    out_ref[...] = scale * total
    low_ref[...] = (scale * total).astype(bf16)


def center_block(scale, turned_rows, weight, group):
    mus, rows, width = turned_rows.shape
    return pl.pallas_call(
        functools.partial(center_kernel, scale, group),
        out_shape=[
            jax.ShapeDtypeStruct((rows, rows), f32),
            jax.ShapeDtypeStruct((rows, rows), bf16),
        ],
        in_specs=spec_all(2),
        out_specs=spec_all(2),
        compiler_params=pltpu.CompilerParams(vmem_limit_bytes=VMEM_BYTES),
        cost_estimate=pl.CostEstimate(
            flops=2 * mus * rows * width * (width + rows) // COST,
            bytes_accessed=2 * mus * rows * width // COST,
            transcendentals=0,
        ),
        name="center",
    )(turned_rows, weight)


def right_kernel(n, kb, spans, leads, groups, first, last, group, scale, *refs):
    fars, refs = refs[: len(spans)], refs[len(spans) :]
    weight_ref, rows_ref = refs[:2]
    refs = refs[2:]
    total = None
    if not first:
        total, refs = refs[0][...], refs[1:]
    outs, flat = refs[:-1], refs[-1]
    mus, cols, width = flat.shape
    nu = width // kb
    start = groups[0] * TILE

    def source(row, line):
        at = (start + line) // TILE * cols + row
        for far, span, lead in zip(fars, spans, leads):
            if span[0] <= at < span[1]:
                return far[lead + at - span[0]]

    def put(line, row, value):
        k = line % kb
        flat[line // kb, row : row + TILE, k * nu : (k + 1) * nu] = value

    turn(source, 0, cols, mus * kb, put)
    for mu in range(0, mus, group):
        lines = flat[mu : mu + group].reshape(group * cols, width)
        turned = mm(lines, weight_ref[...]).astype(bf16)
        left = [
            jnp.concatenate(
                [
                    turned[i * cols : (i + 1) * cols, q * width : (q + 1) * width]
                    for q in range(n)
                ],
                0,
            )
            for i in range(group)
        ]
        part = product(rows_ref, start // kb + mu, group, left)
        total = part if total is None else total + part
    if last:
        for q in range(n):
            outs[q][...] = (scale * total[q * cols : (q + 1) * cols]).astype(bf16)
    else:
        outs[0][...] = total


def right_part(scale, fars, spans, leads, kb, weight, turned_rows, before, groups, last, group):
    _, rows, width = turned_rows.shape
    n = weight.shape[1] // width
    cols = rows // n
    mus = (groups[1] - groups[0]) * TILE // kb
    operands = [*fars, weight, turned_rows]
    if before is not None:
        operands.append(before)
    if last:
        out_shape = [jax.ShapeDtypeStruct((cols, rows), bf16)] * n
    else:
        out_shape = [jax.ShapeDtypeStruct((n * cols, rows), f32)]
    return pl.pallas_call(
        functools.partial(
            right_kernel, n, kb, spans, leads, groups, before is None, last, group, scale
        ),
        out_shape=out_shape,
        in_specs=spec_all(len(operands)),
        out_specs=spec_all(len(out_shape)),
        scratch_shapes=[pltpu.VMEM((mus, cols, width), bf16)],
        compiler_params=pltpu.CompilerParams(vmem_limit_bytes=VMEM_BYTES),
        cost_estimate=pl.CostEstimate(
            flops=2 * mus * cols * n * width * (width + rows) // COST,
            bytes_accessed=2 * mus * rows * width // COST,
            transcendentals=0,
        ),
        name="right",
    )(*operands)


def split(value):
    high = value.astype(bf16)
    return high, (value - high.astype(f32)).astype(bf16)


def upper_kernel(n, pattern, center_ref, even_ref, odd_ref, *refs):
    pieces, (out_ref, middle_ref, masks_ref, right_t, block, sem) = refs[:n], refs[n:]
    me = lax.axis_index("tm")
    cols = pieces[0].shape[0]
    size = center_ref.shape[0]
    for i in range(n):
        start = pl.multiple_of((me ^ i) * cols, cols)
        right_t[pl.ds(start, cols), :] = pieces[i][...]
    parity = lax.axis_index("region") % 2
    above = jnp.where(parity == 0, even_ref[...], odd_ref[...])
    mask = pattern[0, 2].astype(f32)
    upper = right_t[...].T * mask.astype(bf16)
    center = center_ref[...]
    high, low = split(center)
    block[...] = mask * (
        upper.astype(f32) + mm(upper, above) + mm(high, upper) + mm(low, upper)
    )
    copy = pltpu.make_async_copy(block, out_ref.at[0, :, pl.ds(2 * size, size)], sem)
    copy.start()
    middle_ref[...] = (
        center + mm_nt(upper, upper) + mm(high, high) + mm(high, low) + mm(low, high)
    )
    for e in range(2):
        masks_ref[e] = jnp.full(masks_ref.shape[1:], pattern[0, e].astype(f32))
    copy.wait()


def upper_blocks(pattern, center, even, odd, pieces):
    n = len(pieces)
    size = center.shape[0]
    return pl.pallas_call(
        functools.partial(upper_kernel, n),
        out_shape=[
            jax.ShapeDtypeStruct((1, size, 3 * size), f32),
            jax.ShapeDtypeStruct((size, size), f32),
            jax.ShapeDtypeStruct((2, 8, size), f32),
        ],
        in_specs=[SMEM] + spec_all(3 + n),
        out_specs=[HBM] + spec_all(2),
        scratch_shapes=[
            pltpu.VMEM((size, size), bf16),
            pltpu.VMEM((size, size), f32),
            pltpu.SemaphoreType.DMA,
        ],
        compiler_params=pltpu.CompilerParams(vmem_limit_bytes=VMEM_BYTES),
        cost_estimate=pl.CostEstimate(
            flops=16 * size**3 // COST, bytes_accessed=12 * size**2 // COST, transcendentals=0
        ),
        name="upper",
    )(pattern, center, even, odd, *pieces)


def lower_kernel(n, masks_ref, center_ref, middle_ref, even_ref, odd_ref, left_ref, _, out_ref, left, blocks, sems):
    me = lax.axis_index("tm")
    cols = left_ref.shape[1]
    size = center_ref.shape[0]
    for i in range(n):
        start = pl.multiple_of((me ^ i) * cols, cols)
        left[pl.ds(start, cols), :] = left_ref[i]
    parity = lax.axis_index("region") % 2
    below = jnp.where(parity == 0, odd_ref[...], even_ref[...])
    masks = [masks_ref[e, :1, :] for e in range(2)]
    lower = left[...] * masks[0].astype(bf16)
    high, low = split(center_ref[...])
    copies = [
        pltpu.make_async_copy(
            blocks.at[e], out_ref.at[0, :, pl.ds(e * size, size)], sems.at[e]
        )
        for e in range(2)
    ]
    blocks[0] = masks[0] * (
        lower.astype(f32) + mm(lower, below) + mm(high, lower) + mm(low, lower)
    )
    copies[0].start()
    blocks[1] = masks[1] * (middle_ref[...] + mm_nt(lower, lower))
    copies[1].start()
    for copy in copies:
        copy.wait()


def lower_blocks(masks, center, middle, even, odd, left, out):
    n = left.shape[0]
    size = center.shape[0]
    return pl.pallas_call(
        functools.partial(lower_kernel, n),
        out_shape=jax.ShapeDtypeStruct((1, size, 3 * size), f32),
        in_specs=spec_all(6) + [HBM],
        out_specs=HBM,
        input_output_aliases={6: 0},
        scratch_shapes=[
            pltpu.VMEM((size, size), bf16),
            pltpu.VMEM((2, size, size), f32),
            pltpu.SemaphoreType.DMA((2,)),
        ],
        compiler_params=pltpu.CompilerParams(vmem_limit_bytes=VMEM_BYTES),
        cost_estimate=pl.CostEstimate(
            flops=10 * size**3 // COST, bytes_accessed=12 * size**2 // COST, transcendentals=0
        ),
        name="lower",
    )(masks, center, middle, even, odd, left, out)


def local(tensor, g_occ, g_virt, offsets, pattern):
    rows, mus, kb, nu = tensor.shape
    lam = g_occ.shape[2]
    n = lax.axis_size("tm")
    assert n & (n - 1) == 0 and rows % n == 0
    scale = 1.0 / math.sqrt(2.0 * mus * lam) / (3.0 * rows) ** 0.25
    blocks = nu // TILE
    lines = mus * kb
    groups, cols = lines // TILE, rows // n
    cuts = (0, cols, groups * cols)
    spans = tuple(zip(cuts, cuts[1:]))
    lined = tensor.reshape(rows, lines, nu)
    split_rows = lambda x: x.reshape(blocks, TILE, lam)
    own = jnp.concatenate([g_occ[0], g_virt[0]], 0)
    second, below = shift(own, -2), shift(own, 1)
    head, tail, note = prepare(offsets, lined, split_rows(g_occ), split_rows(g_virt), spans, n)
    far_head, far_tail = shift(head, -1), shift(tail, -1)

    size = 2 * nu
    above = far_head[: 2 * blocks]
    stack = jnp.stack([x.reshape(size, lam) for x in (below, own, above, second)], 0)
    turned_rows = relayout(lined, kb, 4)
    greens = {0: stack}
    bit = n // 2
    while bit:
        for i in list(greens):
            if i:
                greens[i], turned_rows = lax.optimization_barrier((greens[i], turned_rows))
            greens[i ^ bit] = partner(greens[i], bit)
        bit //= 2
    center_weight, right_weight = weights(
        note, far_head, 2 * blocks, [greens[i] for i in range(n)]
    )

    center, center_low = center_block(scale, turned_rows, center_weight, 4)

    right_weight, center = lax.optimization_barrier((right_weight, center))
    lead = 2 * blocks + 1
    begun = right_part(
        scale, (far_head,), spans[:1], (lead,), kb, right_weight, turned_rows,
        None, (0, 1), False, 4,
    )
    parts = right_part(
        scale, (far_tail,), spans[1:], (0,), kb, right_weight, turned_rows,
        begun[0], (1, groups), True, 4,
    )
    pieces = dict(enumerate(parts))
    for i in range(n - 1, 0, -1):
        pieces[i] = partner(parts[i], i)
    pieces = [pieces[i] for i in range(n)]
    even, odd = swap_pairs(center_low, 0), swap_pairs(center_low, 1)
    *pieces, even = lax.optimization_barrier((*pieces, even))
    left = shift(jnp.stack(pieces, 0), 1)
    out, middle, masks = upper_blocks(pattern, center, even, odd, pieces)
    return lower_blocks(masks, center, middle, even, odd, left, out)


def solution(mesh):
    return jax.shard_map(
        local,
        mesh=mesh,
        in_specs=(
            P("region", None, None, None),
            P("tm", "region", None),
            P("tm", "region", None),
            P("region", None),
            P("region", None),
        ),
        out_specs=P("tm", "region", None),
        check_vma=False,
    )
```

```python
import functools
import math

import jax
import jax.numpy as jnp
import numpy as np
from jax import lax
from jax.experimental import pallas as pl
from jax.experimental.pallas import tpu as pltpu
from jax.sharding import PartitionSpec as P

time_points = (0.1, 0.5, 1.5, 4.0)
time_weights = (0.2, 0.6, 1.2, 2.5)
omega_points = (0.2, 0.9, 2.5, 7.0)

f32, bf16 = jnp.float32, jnp.bfloat16
VMEM_BYTES = 24 * 2**20
PREPARE_BYTES = 59 * 2**20
RELAYOUT_BYTES = 46 * 2**20
TILE = 16
COST = 3


def cosine_table():
    points = np.array(time_points, np.float32)
    weights = np.array(time_weights, np.float32)
    omegas = np.array(omega_points, np.float32)
    return weights[None, :] * np.cos(omegas[:, None] * points[None, :])


def shift(block, distance):
    devices = range(lax.axis_size("region"))
    route = [(i - distance, i) for i in devices if i - distance in devices]
    return lax.ppermute(block, "region", route)


def swap_pairs(block, first):
    count = lax.axis_size("region")
    route = []
    for i in range(first, count - 1, 2):
        route += [(i, i + 1), (i + 1, i)]
    return lax.ppermute(block, "region", route)


def partner(block, bit):
    return lax.ppermute(block, "tm", [(i, i ^ bit) for i in range(lax.axis_size("tm"))])


def mm(a, b):
    return jnp.dot(a, b, preferred_element_type=f32)


def mm_nt(a, b):
    return lax.dot_general(a, b, (((1,), (1,)), ((), ())), preferred_element_type=f32)


def spec_all(count):
    return [pl.BlockSpec(memory_space=pltpu.VMEM)] * count


SMEM = pl.BlockSpec(memory_space=pltpu.SMEM)
HBM = pl.BlockSpec(memory_space=pltpu.HBM)


def swap_matrix(tile):
    size = tile * tile
    to = lax.broadcasted_iota(jnp.int32, (size, size), 0)
    of = lax.broadcasted_iota(jnp.int32, (size, size), 1)
    return (of == (to % tile) * tile + to // tile).astype(f32).astype(bf16)


def turn(source, lead, rows, lines, put):
    swap = swap_matrix(TILE)
    places = [(r, c) for r in range(0, rows, TILE) for c in range(0, lines, TILE)]
    for at in range(0, len(places), 2):
        pair = places[at : at + 2]
        blocks = [
            jnp.concatenate([source(lead + r + i, c) for i in range(TILE)], 0) for r, c in pair
        ]
        width = blocks[0].shape[1]
        moved = mm(swap, jnp.concatenate(blocks, 1)).astype(bf16)
        for h, (r, c) in enumerate(pair):
            for i in range(TILE):
                put(c + i, r, moved[i * TILE : (i + 1) * TILE, h * width : (h + 1) * width])


def relayout_kernel(kb, chunks, x_ref, out_ref, buffer, sems):
    rows, lines, nu = x_ref.shape
    part = rows // chunks
    copies = [
        pltpu.make_async_copy(
            x_ref.at[pl.ds(c * part, part)], buffer.at[pl.ds(c * part, part)], sems.at[c]
        )
        for c in range(chunks)
    ]
    for copy in copies:
        copy.start()
    for c in range(chunks):
        copies[c].wait()

        def put(line, row, value):
            k = line % kb
            start = c * part + row
            out_ref[line // kb, start : start + TILE, k * nu : (k + 1) * nu] = value

        turn(lambda r, l: buffer[r, l : l + TILE, :], c * part, part, lines, put)


def relayout(lined, kb, chunks):
    rows, lines, nu = lined.shape
    return pl.pallas_call(
        functools.partial(relayout_kernel, kb, chunks),
        out_shape=jax.ShapeDtypeStruct((lines // kb, rows, kb * nu), bf16),
        in_specs=[HBM],
        out_specs=pl.BlockSpec(memory_space=pltpu.VMEM),
        scratch_shapes=[
            pltpu.VMEM((rows, lines, nu), bf16),
            pltpu.SemaphoreType.DMA((chunks,)),
        ],
        compiler_params=pltpu.CompilerParams(vmem_limit_bytes=RELAYOUT_BYTES),
        cost_estimate=pl.CostEstimate(flops=0, bytes_accessed=4 * lined.size // COST, transcendentals=0),
        name="relayout",
    )(lined)


def pieces_of(span, cols):
    runs, at = [], span[0]
    while at < span[1]:
        group, row = divmod(at, cols)
        count = min(cols - row, span[1] - at)
        runs.append((group, row, count, at - span[0]))
        at += count
    return runs


def prepare_kernel(spans, cols, offsets_ref, x_ref, occ_ref, virt_ref, *refs):
    parts, (note_ref, offsets, sems) = refs[: len(spans)], refs[len(spans) :]
    blocks, tile, _ = occ_ref.shape
    mine = lax.axis_index("tm") * cols
    head_ref = parts[0]
    moves = [
        (offsets_ref, offsets),
        (occ_ref, head_ref.at[pl.ds(0, blocks)]),
        (virt_ref, head_ref.at[pl.ds(blocks, blocks)]),
    ]
    for ref, span in zip(parts, spans):
        lead = 2 * blocks + 1 if ref is head_ref else 0
        for group, row, count, place in pieces_of(span, cols):
            source = x_ref.at[pl.ds(mine + row, count), pl.ds(group * tile, tile)]
            moves.append((source, ref.at[pl.ds(lead + place, count)]))
    copies = [pltpu.make_async_copy(*move, sems.at[i]) for i, move in enumerate(moves)]
    for copy in copies:
        copy.start()
    copies[0].wait()
    shape = head_ref.shape[1:]
    line = lax.broadcasted_iota(jnp.int32, shape, 0)
    values = jnp.where(line < shape[0] // 2, offsets[0, 0], offsets[0, 1])
    note_ref[...] = values.astype(f32).astype(bf16)
    head_ref[2 * blocks] = note_ref[...]
    for copy in copies[1:]:
        copy.wait()


def prepare(offsets, lined, occ, virt, spans, n):
    rows, _, nu = lined.shape
    blocks, tile, _ = occ.shape
    cols = rows // n
    tiles = [last - first for first, last in spans]
    tiles[0] += 2 * blocks + 1
    moves = 3 + sum(len(pieces_of(span, cols)) for span in spans)
    return pl.pallas_call(
        functools.partial(prepare_kernel, spans, cols),
        out_shape=[jax.ShapeDtypeStruct((t, tile, nu), bf16) for t in tiles]
        + [jax.ShapeDtypeStruct((tile, nu), bf16)],
        in_specs=[HBM] * 4,
        out_specs=spec_all(len(spans) + 1),
        scratch_shapes=[
            pltpu.SMEM(offsets.shape, jnp.int32),
            pltpu.SemaphoreType.DMA((moves,)),
        ],
        compiler_params=pltpu.CompilerParams(vmem_limit_bytes=PREPARE_BYTES),
        cost_estimate=pl.CostEstimate(flops=0, bytes_accessed=2**20 // COST, transcendentals=0),
        name="prepare",
    )(offsets, lined, occ, virt)


def weights_kernel(n, place, note_ref, head_ref, *refs):
    greens, (center_ref, right_ref, terms) = refs[:n], refs[n:]
    nu = greens[0].shape[1] // 2
    me = lax.axis_index("tm")
    table = cosine_table()

    def weight(frequency, time):
        value = jnp.float32(table[frequency, time])
        for m in range(1, n):
            value = jnp.where(me == m, jnp.float32(table[m ^ frequency, m ^ time]), value)
        return value

    def told(note):
        note = note.astype(f32)
        half = note.shape[0] // 2
        return [jnp.max(note[:half]).astype(jnp.int32), jnp.max(note[half:]).astype(jnp.int32)]

    own = [offset + 1 for offset in told(note_ref[...])]
    following = [offset + 2 for offset in told(head_ref[place])]

    def pick(green, places):
        occ = jnp.concatenate([green[p, :nu, :] for p in places], 0)
        virt = jnp.concatenate([green[p, nu:, :] for p in places], 0)
        return jnp.concatenate([occ, virt], 1), jnp.concatenate([virt, occ], 1)

    center = None
    for i in range(n):
        first, first_swapped = pick(greens[i], own)
        _, second_swapped = pick(greens[i], following)
        term = weight(0, i) * mm_nt(first, first_swapped)
        center = term if center is None else center + term
        terms[i] = mm_nt(second_swapped, first)
    center_ref[...] = center.astype(bf16)
    size = center_ref.shape[0]
    for q in range(n):
        total = weight(q, 0) * terms[0]
        for i in range(1, n):
            total = total + weight(q, i) * terms[i]
        right_ref[:, q * size : (q + 1) * size] = total.astype(bf16)


def weights(note, head, place, greens):
    n = len(greens)
    size = 2 * greens[0].shape[1] // 2
    return pl.pallas_call(
        functools.partial(weights_kernel, n, place),
        out_shape=[
            jax.ShapeDtypeStruct((size, size), bf16),
            jax.ShapeDtypeStruct((size, n * size), bf16),
        ],
        in_specs=spec_all(n + 2),
        out_specs=spec_all(2),
        scratch_shapes=[pltpu.VMEM((n, size, size), f32)],
        compiler_params=pltpu.CompilerParams(vmem_limit_bytes=VMEM_BYTES),
        cost_estimate=pl.CostEstimate(
            flops=4 * n * size**3 // COST, bytes_accessed=n * size**2 * 4 // COST, transcendentals=0
        ),
        name="weights",
    )(note, head, *greens)


def product(rows_ref, first, count, left):
    right = jnp.concatenate([rows_ref[first + i] for i in range(count)], 1)
    return mm_nt(jnp.concatenate(left, 1), right)


def center_kernel(scale, group, rows_ref, weight_ref, out_ref, low_ref):
    mus, rows, width = rows_ref.shape
    total = None
    for first in range(0, mus, group):
        lines = rows_ref[first : first + group].reshape(group * rows, width)
        turned = mm(lines, weight_ref[...]).astype(bf16)
        left = [turned[i * rows : (i + 1) * rows] for i in range(group)]
        part = product(rows_ref, first, group, left)
        total = part if total is None else total + part
    out_ref[...] = scale * total
    low_ref[...] = (scale * total).astype(bf16)


def center_block(scale, turned_rows, weight, group):
    mus, rows, width = turned_rows.shape
    return pl.pallas_call(
        functools.partial(center_kernel, scale, group),
        out_shape=[
            jax.ShapeDtypeStruct((rows, rows), f32),
            jax.ShapeDtypeStruct((rows, rows), bf16),
        ],
        in_specs=spec_all(2),
        out_specs=spec_all(2),
        compiler_params=pltpu.CompilerParams(vmem_limit_bytes=VMEM_BYTES),
        cost_estimate=pl.CostEstimate(
            flops=2 * mus * rows * width * (width + rows) // COST,
            bytes_accessed=2 * mus * rows * width // COST,
            transcendentals=0,
        ),
        name="center",
    )(turned_rows, weight)


def right_kernel(n, kb, spans, leads, groups, first, last, group, scale, *refs):
    fars, refs = refs[: len(spans)], refs[len(spans) :]
    weight_ref, rows_ref = refs[:2]
    refs = refs[2:]
    total = None
    if not first:
        total, refs = refs[0][...], refs[1:]
    outs, flat = refs[:-1], refs[-1]
    mus, cols, width = flat.shape
    nu = width // kb
    start = groups[0] * TILE

    def source(row, line):
        at = (start + line) // TILE * cols + row
        for far, span, lead in zip(fars, spans, leads):
            if span[0] <= at < span[1]:
                return far[lead + at - span[0]]

    def put(line, row, value):
        k = line % kb
        flat[line // kb, row : row + TILE, k * nu : (k + 1) * nu] = value

    turn(source, 0, cols, mus * kb, put)
    for mu in range(0, mus, group):
        lines = flat[mu : mu + group].reshape(group * cols, width)
        turned = mm(lines, weight_ref[...]).astype(bf16)
        left = [
            jnp.concatenate(
                [
                    turned[i * cols : (i + 1) * cols, q * width : (q + 1) * width]
                    for q in range(n)
                ],
                0,
            )
            for i in range(group)
        ]
        part = product(rows_ref, start // kb + mu, group, left)
        total = part if total is None else total + part
    if last:
        for q in range(n):
            outs[q][...] = (scale * total[q * cols : (q + 1) * cols]).astype(bf16)
    else:
        outs[0][...] = total


def right_part(scale, fars, spans, leads, kb, weight, turned_rows, before, groups, last, group):
    _, rows, width = turned_rows.shape
    n = weight.shape[1] // width
    cols = rows // n
    mus = (groups[1] - groups[0]) * TILE // kb
    operands = [*fars, weight, turned_rows]
    if before is not None:
        operands.append(before)
    if last:
        out_shape = [jax.ShapeDtypeStruct((cols, rows), bf16)] * n
    else:
        out_shape = [jax.ShapeDtypeStruct((n * cols, rows), f32)]
    return pl.pallas_call(
        functools.partial(
            right_kernel, n, kb, spans, leads, groups, before is None, last, group, scale
        ),
        out_shape=out_shape,
        in_specs=spec_all(len(operands)),
        out_specs=spec_all(len(out_shape)),
        scratch_shapes=[pltpu.VMEM((mus, cols, width), bf16)],
        compiler_params=pltpu.CompilerParams(vmem_limit_bytes=VMEM_BYTES),
        cost_estimate=pl.CostEstimate(
            flops=2 * mus * cols * n * width * (width + rows) // COST,
            bytes_accessed=2 * mus * rows * width // COST,
            transcendentals=0,
        ),
        name="right",
    )(*operands)


def split(value):
    high = value.astype(bf16)
    return high, (value - high.astype(f32)).astype(bf16)


def upper_kernel(n, pattern, center_ref, even_ref, odd_ref, *refs):
    pieces, (out_ref, middle_ref, masks_ref, right_t, block, sem) = refs[:n], refs[n:]
    me = lax.axis_index("tm")
    cols = pieces[0].shape[0]
    size = center_ref.shape[0]
    for i in range(n):
        start = pl.multiple_of((me ^ i) * cols, cols)
        right_t[pl.ds(start, cols), :] = pieces[i][...]
    parity = lax.axis_index("region") % 2
    above = jnp.where(parity == 0, even_ref[...], odd_ref[...])
    mask = pattern[0, 2].astype(f32)
    upper = right_t[...].T * mask.astype(bf16)
    center = center_ref[...]
    high, low = split(center)
    block[...] = mask * (
        upper.astype(f32) + mm(upper, above) + mm(high, upper) + mm(low, upper)
    )
    copy = pltpu.make_async_copy(block, out_ref.at[0, :, pl.ds(2 * size, size)], sem)
    copy.start()
    middle_ref[...] = (
        center + mm_nt(upper, upper) + mm(high, high) + mm(high, low) + mm(low, high)
    )
    for e in range(2):
        masks_ref[e] = jnp.full(masks_ref.shape[1:], pattern[0, e].astype(f32))
    copy.wait()


def upper_blocks(pattern, center, even, odd, pieces):
    n = len(pieces)
    size = center.shape[0]
    return pl.pallas_call(
        functools.partial(upper_kernel, n),
        out_shape=[
            jax.ShapeDtypeStruct((1, size, 3 * size), f32),
            jax.ShapeDtypeStruct((size, size), f32),
            jax.ShapeDtypeStruct((2, 8, size), f32),
        ],
        in_specs=[SMEM] + spec_all(3 + n),
        out_specs=[HBM] + spec_all(2),
        scratch_shapes=[
            pltpu.VMEM((size, size), bf16),
            pltpu.VMEM((size, size), f32),
            pltpu.SemaphoreType.DMA,
        ],
        compiler_params=pltpu.CompilerParams(vmem_limit_bytes=VMEM_BYTES),
        cost_estimate=pl.CostEstimate(
            flops=16 * size**3 // COST, bytes_accessed=12 * size**2 // COST, transcendentals=0
        ),
        name="upper",
    )(pattern, center, even, odd, *pieces)


def lower_kernel(n, masks_ref, center_ref, middle_ref, even_ref, odd_ref, left_ref, _, out_ref, left, blocks, sems):
    me = lax.axis_index("tm")
    cols = left_ref.shape[1]
    size = center_ref.shape[0]
    for i in range(n):
        start = pl.multiple_of((me ^ i) * cols, cols)
        left[pl.ds(start, cols), :] = left_ref[i]
    parity = lax.axis_index("region") % 2
    below = jnp.where(parity == 0, odd_ref[...], even_ref[...])
    masks = [masks_ref[e, :1, :] for e in range(2)]
    lower = left[...] * masks[0].astype(bf16)
    high, low = split(center_ref[...])
    copies = [
        pltpu.make_async_copy(
            blocks.at[e], out_ref.at[0, :, pl.ds(e * size, size)], sems.at[e]
        )
        for e in range(2)
    ]
    blocks[0] = masks[0] * (
        lower.astype(f32) + mm(lower, below) + mm(high, lower) + mm(low, lower)
    )
    copies[0].start()
    blocks[1] = masks[1] * (middle_ref[...] + mm_nt(lower, lower))
    copies[1].start()
    for copy in copies:
        copy.wait()


def lower_blocks(masks, center, middle, even, odd, left, out):
    n = left.shape[0]
    size = center.shape[0]
    return pl.pallas_call(
        functools.partial(lower_kernel, n),
        out_shape=jax.ShapeDtypeStruct((1, size, 3 * size), f32),
        in_specs=spec_all(6) + [HBM],
        out_specs=HBM,
        input_output_aliases={6: 0},
        scratch_shapes=[
            pltpu.VMEM((size, size), bf16),
            pltpu.VMEM((2, size, size), f32),
            pltpu.SemaphoreType.DMA((2,)),
        ],
        compiler_params=pltpu.CompilerParams(vmem_limit_bytes=VMEM_BYTES),
        cost_estimate=pl.CostEstimate(
            flops=10 * size**3 // COST, bytes_accessed=12 * size**2 // COST, transcendentals=0
        ),
        name="lower",
    )(masks, center, middle, even, odd, left, out)


def local(tensor, g_occ, g_virt, offsets, pattern):
    rows, mus, kb, nu = tensor.shape
    lam = g_occ.shape[2]
    n = lax.axis_size("tm")
    assert n & (n - 1) == 0 and rows % n == 0
    scale = 1.0 / math.sqrt(2.0 * mus * lam) / (3.0 * rows) ** 0.25
    blocks = nu // TILE
    lines = mus * kb
    groups, cols = lines // TILE, rows // n
    cuts = (0, cols, groups * cols)
    spans = tuple(zip(cuts, cuts[1:]))
    lined = tensor.reshape(rows, lines, nu)
    split_rows = lambda x: x.reshape(blocks, TILE, lam)
    own = jnp.concatenate([g_occ[0], g_virt[0]], 0)
    second, below = shift(own, -2), shift(own, 1)
    head, tail, note = prepare(offsets, lined, split_rows(g_occ), split_rows(g_virt), spans, n)
    far_head, far_tail = shift(head, -1), shift(tail, -1)

    size = 2 * nu
    above = far_head[: 2 * blocks]
    stack = jnp.stack([x.reshape(size, lam) for x in (below, own, above, second)], 0)
    turned_rows = relayout(lined, kb, 4)
    greens = {0: stack}
    bit = n // 2
    while bit:
        for i in list(greens):
            if i:
                greens[i], turned_rows = lax.optimization_barrier((greens[i], turned_rows))
            greens[i ^ bit] = partner(greens[i], bit)
        bit //= 2
    center_weight, right_weight = weights(
        note, far_head, 2 * blocks, [greens[i] for i in range(n)]
    )

    center, center_low = center_block(scale, turned_rows, center_weight, 2)

    right_weight, center = lax.optimization_barrier((right_weight, center))
    lead = 2 * blocks + 1
    begun = right_part(
        scale, (far_head,), spans[:1], (lead,), kb, right_weight, turned_rows,
        None, (0, 1), False, 2,
    )
    parts = right_part(
        scale, (far_tail,), spans[1:], (0,), kb, right_weight, turned_rows,
        begun[0], (1, groups), True, 2,
    )
    pieces = dict(enumerate(parts))
    for i in range(n - 1, 0, -1):
        pieces[i] = partner(parts[i], i)
    pieces = [pieces[i] for i in range(n)]
    even, odd = swap_pairs(center_low, 0), swap_pairs(center_low, 1)
    *pieces, even = lax.optimization_barrier((*pieces, even))
    left = shift(jnp.stack(pieces, 0), 1)
    out, middle, masks = upper_blocks(pattern, center, even, odd, pieces)
    return lower_blocks(masks, center, middle, even, odd, left, out)


def solution(mesh):
    return jax.shard_map(
        local,
        mesh=mesh,
        in_specs=(
            P("region", None, None, None),
            P("tm", "region", None),
            P("tm", "region", None),
            P("region", None),
            P("region", None),
        ),
        out_specs=P("tm", "region", None),
        check_vma=False,
    )
```

```python
import functools
import math

import jax
import jax.numpy as jnp
import numpy as np
from jax import lax
from jax.experimental import pallas as pl
from jax.experimental.pallas import tpu as pltpu
from jax.sharding import PartitionSpec as P

time_points = (0.1, 0.5, 1.5, 4.0)
time_weights = (0.2, 0.6, 1.2, 2.5)
omega_points = (0.2, 0.9, 2.5, 7.0)

f32, bf16 = jnp.float32, jnp.bfloat16
VMEM_BYTES = 24 * 2**20
PREPARE_BYTES = 59 * 2**20
RELAYOUT_BYTES = 46 * 2**20
TILE = 16
COST = 3


def cosine_table():
    points = np.array(time_points, np.float32)
    weights = np.array(time_weights, np.float32)
    omegas = np.array(omega_points, np.float32)
    return weights[None, :] * np.cos(omegas[:, None] * points[None, :])


def shift(block, distance):
    devices = range(lax.axis_size("region"))
    route = [(i - distance, i) for i in devices if i - distance in devices]
    return lax.ppermute(block, "region", route)


def swap_pairs(block, first):
    count = lax.axis_size("region")
    route = []
    for i in range(first, count - 1, 2):
        route += [(i, i + 1), (i + 1, i)]
    return lax.ppermute(block, "region", route)


def partner(block, bit):
    return lax.ppermute(block, "tm", [(i, i ^ bit) for i in range(lax.axis_size("tm"))])


def mm(a, b):
    return jnp.dot(a, b, preferred_element_type=f32)


def mm_nt(a, b):
    return lax.dot_general(a, b, (((1,), (1,)), ((), ())), preferred_element_type=f32)


def spec_all(count):
    return [pl.BlockSpec(memory_space=pltpu.VMEM)] * count


SMEM = pl.BlockSpec(memory_space=pltpu.SMEM)
HBM = pl.BlockSpec(memory_space=pltpu.HBM)


def swap_matrix(tile):
    size = tile * tile
    to = lax.broadcasted_iota(jnp.int32, (size, size), 0)
    of = lax.broadcasted_iota(jnp.int32, (size, size), 1)
    return (of == (to % tile) * tile + to // tile).astype(f32).astype(bf16)


def turn(source, lead, rows, lines, put):
    swap = swap_matrix(TILE)
    places = [(r, c) for r in range(0, rows, TILE) for c in range(0, lines, TILE)]
    for at in range(0, len(places), 4):
        pair = places[at : at + 4]
        blocks = [
            jnp.concatenate([source(lead + r + i, c) for i in range(TILE)], 0) for r, c in pair
        ]
        width = blocks[0].shape[1]
        moved = mm(swap, jnp.concatenate(blocks, 1)).astype(bf16)
        for h, (r, c) in enumerate(pair):
            for i in range(TILE):
                put(c + i, r, moved[i * TILE : (i + 1) * TILE, h * width : (h + 1) * width])


def relayout_kernel(kb, chunks, x_ref, out_ref, buffer, sems):
    rows, lines, nu = x_ref.shape
    part = rows // chunks
    copies = [
        pltpu.make_async_copy(
            x_ref.at[pl.ds(c * part, part)], buffer.at[pl.ds(c * part, part)], sems.at[c]
        )
        for c in range(chunks)
    ]
    for copy in copies:
        copy.start()
    for c in range(chunks):
        copies[c].wait()

        def put(line, row, value):
            k = line % kb
            start = c * part + row
            out_ref[line // kb, start : start + TILE, k * nu : (k + 1) * nu] = value

        turn(lambda r, l: buffer[r, l : l + TILE, :], c * part, part, lines, put)


def relayout(lined, kb, chunks):
    rows, lines, nu = lined.shape
    return pl.pallas_call(
        functools.partial(relayout_kernel, kb, chunks),
        out_shape=jax.ShapeDtypeStruct((lines // kb, rows, kb * nu), bf16),
        in_specs=[HBM],
        out_specs=pl.BlockSpec(memory_space=pltpu.VMEM),
        scratch_shapes=[
            pltpu.VMEM((rows, lines, nu), bf16),
            pltpu.SemaphoreType.DMA((chunks,)),
        ],
        compiler_params=pltpu.CompilerParams(vmem_limit_bytes=RELAYOUT_BYTES),
        cost_estimate=pl.CostEstimate(flops=0, bytes_accessed=4 * lined.size // COST, transcendentals=0),
        name="relayout",
    )(lined)


def pieces_of(span, cols):
    runs, at = [], span[0]
    while at < span[1]:
        group, row = divmod(at, cols)
        count = min(cols - row, span[1] - at)
        runs.append((group, row, count, at - span[0]))
        at += count
    return runs


def prepare_kernel(spans, cols, offsets_ref, x_ref, occ_ref, virt_ref, *refs):
    parts, (note_ref, offsets, sems) = refs[: len(spans)], refs[len(spans) :]
    blocks, tile, _ = occ_ref.shape
    mine = lax.axis_index("tm") * cols
    head_ref = parts[0]
    moves = [
        (offsets_ref, offsets),
        (occ_ref, head_ref.at[pl.ds(0, blocks)]),
        (virt_ref, head_ref.at[pl.ds(blocks, blocks)]),
    ]
    for ref, span in zip(parts, spans):
        lead = 2 * blocks + 1 if ref is head_ref else 0
        for group, row, count, place in pieces_of(span, cols):
            source = x_ref.at[pl.ds(mine + row, count), pl.ds(group * tile, tile)]
            moves.append((source, ref.at[pl.ds(lead + place, count)]))
    copies = [pltpu.make_async_copy(*move, sems.at[i]) for i, move in enumerate(moves)]
    for copy in copies:
        copy.start()
    copies[0].wait()
    shape = head_ref.shape[1:]
    line = lax.broadcasted_iota(jnp.int32, shape, 0)
    values = jnp.where(line < shape[0] // 2, offsets[0, 0], offsets[0, 1])
    note_ref[...] = values.astype(f32).astype(bf16)
    head_ref[2 * blocks] = note_ref[...]
    for copy in copies[1:]:
        copy.wait()


def prepare(offsets, lined, occ, virt, spans, n):
    rows, _, nu = lined.shape
    blocks, tile, _ = occ.shape
    cols = rows // n
    tiles = [last - first for first, last in spans]
    tiles[0] += 2 * blocks + 1
    moves = 3 + sum(len(pieces_of(span, cols)) for span in spans)
    return pl.pallas_call(
        functools.partial(prepare_kernel, spans, cols),
        out_shape=[jax.ShapeDtypeStruct((t, tile, nu), bf16) for t in tiles]
        + [jax.ShapeDtypeStruct((tile, nu), bf16)],
        in_specs=[HBM] * 4,
        out_specs=spec_all(len(spans) + 1),
        scratch_shapes=[
            pltpu.SMEM(offsets.shape, jnp.int32),
            pltpu.SemaphoreType.DMA((moves,)),
        ],
        compiler_params=pltpu.CompilerParams(vmem_limit_bytes=PREPARE_BYTES),
        cost_estimate=pl.CostEstimate(flops=0, bytes_accessed=2**20 // COST, transcendentals=0),
        name="prepare",
    )(offsets, lined, occ, virt)


def weights_kernel(n, place, note_ref, head_ref, *refs):
    greens, (center_ref, right_ref, terms) = refs[:n], refs[n:]
    nu = greens[0].shape[1] // 2
    me = lax.axis_index("tm")
    table = cosine_table()

    def weight(frequency, time):
        value = jnp.float32(table[frequency, time])
        for m in range(1, n):
            value = jnp.where(me == m, jnp.float32(table[m ^ frequency, m ^ time]), value)
        return value

    def told(note):
        note = note.astype(f32)
        half = note.shape[0] // 2
        return [jnp.max(note[:half]).astype(jnp.int32), jnp.max(note[half:]).astype(jnp.int32)]

    own = [offset + 1 for offset in told(note_ref[...])]
    following = [offset + 2 for offset in told(head_ref[place])]

    def pick(green, places):
        occ = jnp.concatenate([green[p, :nu, :] for p in places], 0)
        virt = jnp.concatenate([green[p, nu:, :] for p in places], 0)
        return jnp.concatenate([occ, virt], 1), jnp.concatenate([virt, occ], 1)

    center = None
    for i in range(n):
        first, first_swapped = pick(greens[i], own)
        _, second_swapped = pick(greens[i], following)
        term = weight(0, i) * mm_nt(first, first_swapped)
        center = term if center is None else center + term
        terms[i] = mm_nt(second_swapped, first)
    center_ref[...] = center.astype(bf16)
    size = center_ref.shape[0]
    for q in range(n):
        total = weight(q, 0) * terms[0]
        for i in range(1, n):
            total = total + weight(q, i) * terms[i]
        right_ref[:, q * size : (q + 1) * size] = total.astype(bf16)


def weights(note, head, place, greens):
    n = len(greens)
    size = 2 * greens[0].shape[1] // 2
    return pl.pallas_call(
        functools.partial(weights_kernel, n, place),
        out_shape=[
            jax.ShapeDtypeStruct((size, size), bf16),
            jax.ShapeDtypeStruct((size, n * size), bf16),
        ],
        in_specs=spec_all(n + 2),
        out_specs=spec_all(2),
        scratch_shapes=[pltpu.VMEM((n, size, size), f32)],
        compiler_params=pltpu.CompilerParams(vmem_limit_bytes=VMEM_BYTES),
        cost_estimate=pl.CostEstimate(
            flops=4 * n * size**3 // COST, bytes_accessed=n * size**2 * 4 // COST, transcendentals=0
        ),
        name="weights",
    )(note, head, *greens)


def product(rows_ref, first, count, left):
    right = jnp.concatenate([rows_ref[first + i] for i in range(count)], 1)
    return mm_nt(jnp.concatenate(left, 1), right)


def center_kernel(scale, group, rows_ref, weight_ref, out_ref, low_ref, quarters_ref):
    mus, rows, width = rows_ref.shape
    total = None
    for first in range(0, mus, group):
        lines = rows_ref[first : first + group].reshape(group * rows, width)
        turned = mm(lines, weight_ref[...]).astype(bf16)
        left = [turned[i * rows : (i + 1) * rows] for i in range(group)]
        part = product(rows_ref, first, group, left)
        total = part if total is None else total + part
    out_ref[...] = scale * total
    low = (scale * total).astype(bf16)
    half = rows // 2
    low_ref[...] = low
    quarters_ref[0] = low[:half, :half]
    quarters_ref[1] = low[:half, half:]
    quarters_ref[2] = low[half:, half:]


def center_block(scale, turned_rows, weight, group):
    mus, rows, width = turned_rows.shape
    half = rows // 2
    return pl.pallas_call(
        functools.partial(center_kernel, scale, group),
        out_shape=[
            jax.ShapeDtypeStruct((rows, rows), f32),
            jax.ShapeDtypeStruct((rows, rows), bf16),
            jax.ShapeDtypeStruct((3, half, half), bf16),
        ],
        in_specs=spec_all(2),
        out_specs=spec_all(3),
        compiler_params=pltpu.CompilerParams(vmem_limit_bytes=VMEM_BYTES),
        cost_estimate=pl.CostEstimate(
            flops=2 * mus * rows * width * (width + rows) // COST,
            bytes_accessed=2 * mus * rows * width // COST,
            transcendentals=0,
        ),
        name="center",
    )(turned_rows, weight)


def right_kernel(n, kb, spans, leads, groups, first, last, group, scale, *refs):
    fars, refs = refs[: len(spans)], refs[len(spans) :]
    weight_ref, rows_ref = refs[:2]
    refs = refs[2:]
    total = None
    if not first:
        total, refs = refs[0][...], refs[1:]
    outs, flat = refs[:-1], refs[-1]
    mus, cols, width = flat.shape
    nu = width // kb
    start = groups[0] * TILE

    def source(row, line):
        at = (start + line) // TILE * cols + row
        for far, span, lead in zip(fars, spans, leads):
            if span[0] <= at < span[1]:
                return far[lead + at - span[0]]

    def put(line, row, value):
        k = line % kb
        flat[line // kb, row : row + TILE, k * nu : (k + 1) * nu] = value

    turn(source, 0, cols, mus * kb, put)
    for mu in range(0, mus, group):
        lines = flat[mu : mu + group].reshape(group * cols, width)
        turned = mm(lines, weight_ref[...]).astype(bf16)
        left = [
            jnp.concatenate(
                [
                    turned[i * cols : (i + 1) * cols, q * width : (q + 1) * width]
                    for q in range(n)
                ],
                0,
            )
            for i in range(group)
        ]
        part = product(rows_ref, start // kb + mu, group, left)
        total = part if total is None else total + part
    if last:
        for q in range(n):
            outs[q][...] = (scale * total[q * cols : (q + 1) * cols]).astype(bf16)
    else:
        outs[0][...] = total


def right_part(scale, fars, spans, leads, kb, weight, turned_rows, before, groups, last, group):
    _, rows, width = turned_rows.shape
    n = weight.shape[1] // width
    cols = rows // n
    mus = (groups[1] - groups[0]) * TILE // kb
    operands = [*fars, weight, turned_rows]
    if before is not None:
        operands.append(before)
    if last:
        out_shape = [jax.ShapeDtypeStruct((cols, rows), bf16)] * n
    else:
        out_shape = [jax.ShapeDtypeStruct((n * cols, rows), f32)]
    return pl.pallas_call(
        functools.partial(
            right_kernel, n, kb, spans, leads, groups, before is None, last, group, scale
        ),
        out_shape=out_shape,
        in_specs=spec_all(len(operands)),
        out_specs=spec_all(len(out_shape)),
        scratch_shapes=[pltpu.VMEM((mus, cols, width), bf16)],
        compiler_params=pltpu.CompilerParams(vmem_limit_bytes=VMEM_BYTES),
        cost_estimate=pl.CostEstimate(
            flops=2 * mus * cols * n * width * (width + rows) // COST,
            bytes_accessed=2 * mus * rows * width // COST,
            transcendentals=0,
        ),
        name="right",
    )(*operands)


def split(value):
    high = value.astype(bf16)
    return high, (value - high.astype(f32)).astype(bf16)


def whole_block(quarters):
    first, second, last = quarters[0], quarters[1], quarters[2]
    return jnp.concatenate(
        [jnp.concatenate([first, second], 1), jnp.concatenate([second.T, last], 1)], 0
    )


def upper_kernel(n, pattern, center_ref, even_ref, odd_ref, *refs):
    pieces, (out_ref, middle_ref, masks_ref, right_t, block, sem) = refs[:n], refs[n:]
    me = lax.axis_index("tm")
    cols = pieces[0].shape[0]
    size = center_ref.shape[0]
    for i in range(n):
        start = pl.multiple_of((me ^ i) * cols, cols)
        right_t[pl.ds(start, cols), :] = pieces[i][...]
    parity = lax.axis_index("region") % 2
    above = jnp.where(parity == 0, whole_block(even_ref), odd_ref[...])
    mask = pattern[0, 2].astype(f32)
    upper = right_t[...].T * mask.astype(bf16)
    center = center_ref[...]
    high, low = split(center)
    block[...] = mask * (
        upper.astype(f32) + mm(upper, above) + mm(high, upper) + mm(low, upper)
    )
    copy = pltpu.make_async_copy(block, out_ref.at[0, :, pl.ds(2 * size, size)], sem)
    copy.start()
    middle_ref[...] = (
        center + mm_nt(upper, upper) + mm(high, high) + mm(high, low) + mm(low, high)
    )
    for e in range(2):
        masks_ref[e] = jnp.full(masks_ref.shape[1:], pattern[0, e].astype(f32))
    copy.wait()


def upper_blocks(pattern, center, even, odd, pieces):
    n = len(pieces)
    size = center.shape[0]
    return pl.pallas_call(
        functools.partial(upper_kernel, n),
        out_shape=[
            jax.ShapeDtypeStruct((1, size, 3 * size), f32),
            jax.ShapeDtypeStruct((size, size), f32),
            jax.ShapeDtypeStruct((2, 8, size), f32),
        ],
        in_specs=[SMEM] + spec_all(3 + n),
        out_specs=[HBM] + spec_all(2),
        scratch_shapes=[
            pltpu.VMEM((size, size), bf16),
            pltpu.VMEM((size, size), f32),
            pltpu.SemaphoreType.DMA,
        ],
        compiler_params=pltpu.CompilerParams(vmem_limit_bytes=VMEM_BYTES),
        cost_estimate=pl.CostEstimate(
            flops=16 * size**3 // COST, bytes_accessed=12 * size**2 // COST, transcendentals=0
        ),
        name="upper",
    )(pattern, center, even, odd, *pieces)


def lower_kernel(n, masks_ref, center_ref, middle_ref, even_ref, odd_ref, left_ref, _, out_ref, left, blocks, sems):
    me = lax.axis_index("tm")
    cols = left_ref.shape[1]
    size = center_ref.shape[0]
    for i in range(n):
        start = pl.multiple_of((me ^ i) * cols, cols)
        left[pl.ds(start, cols), :] = left_ref[i]
    parity = lax.axis_index("region") % 2
    below = jnp.where(parity == 0, odd_ref[...], whole_block(even_ref))
    masks = [masks_ref[e, :1, :] for e in range(2)]
    lower = left[...] * masks[0].astype(bf16)
    high, low = split(center_ref[...])
    copies = [
        pltpu.make_async_copy(
            blocks.at[e], out_ref.at[0, :, pl.ds(e * size, size)], sems.at[e]
        )
        for e in range(2)
    ]
    blocks[0] = masks[0] * (
        lower.astype(f32) + mm(lower, below) + mm(high, lower) + mm(low, lower)
    )
    copies[0].start()
    blocks[1] = masks[1] * (middle_ref[...] + mm_nt(lower, lower))
    copies[1].start()
    for copy in copies:
        copy.wait()


def lower_blocks(masks, center, middle, even, odd, left, out):
    n = left.shape[0]
    size = center.shape[0]
    return pl.pallas_call(
        functools.partial(lower_kernel, n),
        out_shape=jax.ShapeDtypeStruct((1, size, 3 * size), f32),
        in_specs=spec_all(6) + [HBM],
        out_specs=HBM,
        input_output_aliases={6: 0},
        scratch_shapes=[
            pltpu.VMEM((size, size), bf16),
            pltpu.VMEM((2, size, size), f32),
            pltpu.SemaphoreType.DMA((2,)),
        ],
        compiler_params=pltpu.CompilerParams(vmem_limit_bytes=VMEM_BYTES),
        cost_estimate=pl.CostEstimate(
            flops=10 * size**3 // COST, bytes_accessed=12 * size**2 // COST, transcendentals=0
        ),
        name="lower",
    )(masks, center, middle, even, odd, left, out)


def local(tensor, g_occ, g_virt, offsets, pattern):
    rows, mus, kb, nu = tensor.shape
    lam = g_occ.shape[2]
    n = lax.axis_size("tm")
    assert n & (n - 1) == 0 and rows % n == 0
    scale = 1.0 / math.sqrt(2.0 * mus * lam) / (3.0 * rows) ** 0.25
    blocks = nu // TILE
    lines = mus * kb
    groups, cols = lines // TILE, rows // n
    cuts = (0, cols, groups * cols)
    spans = tuple(zip(cuts, cuts[1:]))
    lined = tensor.reshape(rows, lines, nu)
    split_rows = lambda x: x.reshape(blocks, TILE, lam)
    own = jnp.concatenate([g_occ[0], g_virt[0]], 0)
    second, below = shift(own, -2), shift(own, 1)
    head, tail, note = prepare(offsets, lined, split_rows(g_occ), split_rows(g_virt), spans, n)
    far_head, far_tail = shift(head, -1), shift(tail, -1)

    size = 2 * nu
    above = far_head[: 2 * blocks]
    stack = jnp.stack([x.reshape(size, lam) for x in (below, own, above, second)], 0)
    turned_rows = relayout(lined, kb, 4)
    greens = {0: stack}
    bit = n // 2
    while bit:
        for i in list(greens):
            if i:
                greens[i], turned_rows = lax.optimization_barrier((greens[i], turned_rows))
            greens[i ^ bit] = partner(greens[i], bit)
        bit //= 2
    center_weight, right_weight = weights(
        note, far_head, 2 * blocks, [greens[i] for i in range(n)]
    )

    center, center_low, quarters = center_block(scale, turned_rows, center_weight, 2)

    right_weight, center = lax.optimization_barrier((right_weight, center))
    lead = 2 * blocks + 1
    begun = right_part(
        scale, (far_head,), spans[:1], (lead,), kb, right_weight, turned_rows,
        None, (0, 1), False, 2,
    )
    parts = right_part(
        scale, (far_tail,), spans[1:], (0,), kb, right_weight, turned_rows,
        begun[0], (1, groups), True, 2,
    )
    pieces = dict(enumerate(parts))
    for i in range(n - 1, 0, -1):
        pieces[i] = partner(parts[i], i)
    pieces = [pieces[i] for i in range(n)]
    even, odd = swap_pairs(quarters, 0), swap_pairs(center_low, 1)
    *pieces, even = lax.optimization_barrier((*pieces, even))
    left = shift(jnp.stack(pieces, 0), 1)
    out, middle, masks = upper_blocks(pattern, center, even, odd, pieces)
    return lower_blocks(masks, center, middle, even, odd, left, out)


def solution(mesh):
    return jax.shard_map(
        local,
        mesh=mesh,
        in_specs=(
            P("region", None, None, None),
            P("tm", "region", None),
            P("tm", "region", None),
            P("region", None),
            P("region", None),
        ),
        out_specs=P("tm", "region", None),
        check_vma=False,
    )
```
